512 devices in a mesh: shot: 8 (over z_lo, core), space: 64 (over y, z_hi, x).
Axes of the slice: x: 4, y: 8, z: 8 (z_hi: 2, z_lo: 4; z = z_hi * 4 + z_lo), core: 2. Of those that a mesh axis runs over, the one named last changes fastest.
Arguments:
- velocity_term: float32 [512, 64, 128], P('space'), may hold values from 0.05 to 0.2
- forward_previous: float32 [8, 512, 64, 128], P('shot', 'space'), may hold values from -6 to 6
- forward_current: float32 [8, 512, 64, 128], P('shot', 'space'), may hold values from -6 to 6
- adjoint_previous: float32 [8, 512, 64, 128], P('shot', 'space'), may hold values from -6 to 6
- adjoint_current: float32 [8, 512, 64, 128], P('shot', 'space'), may hold values from -6 to 6
- source_cell: int32 [8], P('shot'), may hold values from 0 to 4194303
- wavelet: float32 [8, 2], P('shot'), may hold values from -40 to 40
- trace_cells: int32 [8, 512, 8], P('shot'), may hold values from 0 to 4194303, as said below
- trace_weights: float32 [8, 512, 8], P('shot'), may hold values from -2 to 2
- observed: float32 [8, 2, 512], P('shot', None, 'space'), may hold values from -6 to 6
Outputs:
- forward_next: float32 [8, 512, 64, 128], P('shot', 'space')
- adjoint_next: float32 [8, 512, 64, 128], P('shot', 'space')
- residual: float32 [8, 2, 512], P('shot', None, 'space')
- gradient: float32 [512, 64, 128], P('space', 'shot')
The draws below stay inside these ranges and needn't reach their ends.
Inputs may be any that keep to these rules, and one draw needn't show every extreme that they name: `trace_cells`: each trace's footprint is 8 cells in a row along the first dimension at one position of the other two; a trace lies in the first quarter of the first dimension with chance about one half.
All inputs are finite; a program needn't handle non-finite values.
Results may differ from the reference program's by a relative error of at most 0.0001.
Values sent between devices are 32-bit elements; how exact they have to be, the bound alone decides.
A program may use at most 64 MiB of HBM per device.

```python
import math
import jax
import jax.numpy as jnp

NY = 64
NZ = 128
TAPS = 8
NX = 512
SHOTS = 8
TRACES = 512


def draw_trace_cells(key, part):
    key_coin = jax.random.fold_in(key, 11)
    key_near = jax.random.fold_in(key, 12)
    key_far = jax.random.fold_in(key, 13)
    key_y = jax.random.fold_in(key, 14)
    key_z = jax.random.fold_in(key, 15)
    coin = jax.random.randint(key_coin, (SHOTS, TRACES), 0, 2)
    near = jax.random.randint(key_near, (SHOTS, TRACES), 0, NX // 4 - TAPS + 1)
    far = jax.random.randint(key_far, (SHOTS, TRACES), NX // 4, NX - TAPS + 1)
    start_x = jnp.where(coin == 1, near, far)
    pos_y = jax.random.randint(key_y, (SHOTS, TRACES), 0, NY)
    pos_z = jax.random.randint(key_z, (SHOTS, TRACES), 0, NZ)
    start_x = start_x.at[:, 0].set(NX - TAPS).at[:, 1].set(0)
    pos_y = pos_y.at[:, 0].set(NY - 1).at[:, 1].set(0)
    pos_z = pos_z.at[:, 0].set(NZ - 1).at[:, 1].set(0)
    taps_x = start_x[:, :, None] + jnp.arange(TAPS, dtype=jnp.int32)[None, None, :]
    flat = (taps_x * NY + pos_y[:, :, None]) * NZ + pos_z[:, :, None]
    return flat.astype(jnp.int32)


def set_ends(drawn, own_key, low, largest):
    shape = drawn.shape
    spot = [jax.random.randint(jax.random.fold_in(own_key, axis), (), 0, shape[axis]) for axis in range(len(shape))]
    drawn = drawn.at[tuple(spot)].set(low)
    longest = shape.index(max(shape))
    spot[longest] = (spot[longest] + 1) % shape[longest]
    return drawn.at[tuple(spot)].set(largest)


def block_levels(stream_key, shape, shards, least, largest):
    factor_of, own = 1.0, jax.random.fold_in(stream_key, 6)
    for position, parts in shards:
        heights = jnp.exp(jax.random.uniform(jax.random.fold_in(own, position), (parts,), jnp.float32, least / len(shards), largest / len(shards)))
        factor_of = factor_of * jnp.repeat(heights, shape[position] // parts).reshape([-1 if axis == position else 1 for axis in range(len(shape))])
    return factor_of


def scatter_about(key, shape, width, limit, pieces=(), kind=jnp.bfloat16):
    values = jax.random.normal(key, shape, jnp.float32) * width
    if len(pieces) > 0:
        values = block_levels(key, shape, pieces, -0.22, 0.18) * values
    return jnp.clip(values, min=-limit, max=limit).astype(kind)


def setup_inputs(seed: int = 0) -> dict:
    seeds = jax.random.split(jax.random.key(seed), 11)
    return {
        "velocity_term": jnp.clip(jnp.exp(math.log(0.2) - 1.3862944 * jax.random.uniform(seeds[0], (NX, NY, NZ), jnp.float32) ** block_levels(seeds[0], (NX, NY, NZ), ((0, 64),), -0.2, 0.2)), 0.05, 0.2),
        "forward_previous": scatter_about(seeds[1], (SHOTS, NX, NY, NZ), 1.0, 6.0, ((0, 8), (1, 64)), jnp.float32),
        "forward_current": scatter_about(seeds[2], (SHOTS, NX, NY, NZ), 1.0, 6.0, ((0, 8), (1, 64)), jnp.float32),
        "adjoint_previous": scatter_about(seeds[3], (SHOTS, NX, NY, NZ), 1.0, 6.0, ((0, 8), (1, 64)), jnp.float32),
        "adjoint_current": scatter_about(seeds[4], (SHOTS, NX, NY, NZ), 1.0, 6.0, ((0, 8), (1, 64)), jnp.float32),
        "source_cell": set_ends(jax.random.randint(seeds[5], (SHOTS,), 0, NX * NY * NZ), jax.random.fold_in(seeds[5], 1), 0, (NX * NY * NZ) - 1).astype(jnp.int32),
        "wavelet": scatter_about(seeds[6], (SHOTS, 2), 10.0, 40.0, ((0, 8),), jnp.float32),
        "trace_cells": draw_trace_cells(jax.random.fold_in(seeds[10], 71), 0),
        "trace_weights": scatter_about(seeds[8], (SHOTS, TRACES, TAPS), 0.35, 2.0, ((0, 8),), jnp.float32),
        "observed": scatter_about(seeds[9], (SHOTS, 2, TRACES), 1.0, 6.0, ((0, 8), (2, 64)), jnp.float32),
    }


coeffs = (-205.0 / 72.0, 8.0 / 5.0, -1.0 / 5.0, 8.0 / 315.0, -1.0 / 560.0)


def laplace_ext(field):
    count = field.shape[0] - 8
    core = field[4:4 + count]
    width_y = core.shape[1]
    width_z = core.shape[2]
    padded = jnp.pad(core, ((0, 0), (4, 4), (4, 4)))
    result = 3.0 * coeffs[0] * core
    for j in range(1, 5):
        along_x = field[4 + j:4 + j + count] + field[4 - j:4 - j + count]
        along_y = padded[:, 4 + j:4 + j + width_y, 4:4 + width_z] + padded[:, 4 - j:4 - j + width_y, 4:4 + width_z]
        along_z = padded[:, 4:4 + width_y, 4 + j:4 + j + width_z] + padded[:, 4:4 + width_y, 4 - j:4 - j + width_z]
        result = result + coeffs[j] * (along_x + along_y + along_z)
    return result


def laplace(field):
    return laplace_ext(jnp.pad(field, ((4, 4), (0, 0), (0, 0))))


def reference(velocity_term, forward_previous, forward_current, adjoint_previous, adjoint_current, source_cell, wavelet, trace_cells, trace_weights, observed):
    shape = velocity_term.shape
    speed_flat = velocity_term.reshape(-1)
    gradient = jnp.zeros(shape, jnp.float32)
    outs_forward = []
    outs_adjoint = []
    outs_residual = []
    for shot_index in range(SHOTS):
        cells = trace_cells[shot_index]
        weights = trace_weights[shot_index]

        def add_source(field, amount):
            place = source_cell[shot_index]
            return field.reshape(-1).at[place].add(speed_flat[place] * amount).reshape(shape)

        def sample(field):
            return jnp.sum(field.reshape(-1)[cells] * weights, axis=-1)

        def add_inject(field, values):
            flat_cells = cells.reshape(-1)
            amounts = (weights * values[:, None]).reshape(-1) * speed_flat[flat_cells]
            return field.reshape(-1).at[flat_cells].add(amounts).reshape(shape)

        p_before = forward_previous[shot_index]
        p_now = forward_current[shot_index]
        lap_zero = laplace(p_now)
        p_one = add_source(2.0 * p_now - p_before + velocity_term * lap_zero, wavelet[shot_index, 0])
        lap_one = laplace(p_one)
        p_two = add_source(2.0 * p_one - p_now + velocity_term * lap_one, wavelet[shot_index, 1])
        synthetic = jnp.stack([sample(p_one), sample(p_two)])
        misfit = synthetic - observed[shot_index]
        a_before = adjoint_previous[shot_index]
        a_now = adjoint_current[shot_index]
        a_one = add_inject(2.0 * a_now - a_before + velocity_term * laplace(a_now), misfit[1])
        a_two = add_inject(2.0 * a_one - a_now + velocity_term * laplace(a_one), misfit[0])
        gradient = gradient + a_one * lap_one + a_two * lap_zero
        outs_forward.append(p_two)
        outs_adjoint.append(a_two)
        outs_residual.append(misfit)
    return jnp.stack(outs_forward), jnp.stack(outs_adjoint), jnp.stack(outs_residual), gradient * (1.0 / SHOTS)
```

```python
import functools

import jax
import jax.numpy as jnp
from jax import lax
from jax.experimental import pallas as pl
from jax.experimental.pallas import tpu as pltpu
from jax.sharding import PartitionSpec as P

MESH = pl.DeviceIdType.MESH
F32, BF16 = jnp.float32, jnp.bfloat16
coeffs = (-205.0 / 72.0, 8.0 / 5.0, -1.0 / 5.0, 8.0 / 315.0, -1.0 / 560.0)
whole = (8064.0, -1008.0, 128.0, -9.0)


def split(f):
    hi = f.astype(BF16)
    return hi, (f - hi.astype(F32)).astype(BF16)


def dot(a, b):
    return jnp.dot(a, b, preferred_element_type=F32)


def band(i, j):
    d = jnp.abs(i - j)
    m = jnp.zeros(d.shape, F32)
    for k, c in enumerate(whole):
        m = jnp.where(d == k + 1, c, m)
    return m.astype(BF16)


def iota(shape, dim):
    return lax.broadcasted_iota(jnp.int32, shape, dim)


def lap_inside(f, dz, dy):
    rows, ny, nz = f.shape
    hi, lo = split(f)
    zz = dot(jnp.concatenate([hi.reshape(rows * ny, nz), lo.reshape(rows * ny, nz)], axis=1), dz)
    yy = dot(dy, jnp.concatenate([jnp.concatenate([hi[x], lo[x]], axis=0) for x in range(rows)], axis=1))
    out = []
    for x in range(rows):
        r = 3.0 * coeffs[0] * f[x] + (zz[x * ny : (x + 1) * ny] + yy[:, x * nz : (x + 1) * nz]) * (1.0 / 5040.0)
        for j in range(1, 5):
            terms = [f[k] for k in (x - j, x + j) if 0 <= k < rows]
            if terms:
                r = r + coeffs[j] * functools.reduce(jnp.add, terms)
        out.append(r)
    return out


def from_left(h, i, edge):
    return functools.reduce(jnp.add, [(coeffs[j] * edge) * h[4 + i - j] for j in range(i + 1, 5)])


def from_right(h, i, edge):
    return functools.reduce(jnp.add, [(coeffs[j] * edge) * h[i + j - 4] for j in range(4 - i, 5)])


def kernel(
    sizes,
    v_in, pm_in, p0_in, am_in, a0_in, cell_in, wave_in, cells_in, weights_in, obs_in,
    f_out, a_out, r_out, g_out,
    V, PM, P0, AM, A0, LAP0, P1, LAP1, P2, A1, A2, INJ0, terms, grad,
    cell, wave, cells, weights, obs, obs_wide, res,
    halo, ozT, oz, oyT, wx, dz, dy,
    part, part_in, arow, sums, sums_y, sums_z, sums_x, gin,
    load_sem, out_sem, send_sem, recv_sem,
):
    n_shot, n_space, nx_, nz_, ny_ = sizes
    rows, ny, nz = V.shape
    traces = weights.shape[1]
    blocks = traces // 128
    h = lax.axis_index("shot")
    s = lax.axis_index("space")
    x, zh, y = s % nx_, (s // nx_) % nz_, s // (nx_ * nz_)

    def ring(k):
        return (h, (s + k + n_space) % n_space)

    def slab(x, zh, y):
        return (h, (y * nz_ + zh) * nx_ + x)

    to_y = [slab(x, zh, (y + k) % ny_) for k in range(1, ny_)]
    to_z = [slab(x, (zh + k) % nz_, y) for k in range(1, nz_)]
    to_x = [slab((x + k) % nx_, zh, y) for k in range(1, nx_)]
    to_shot = [((h + k) % n_shot, s) for k in range(1, n_shot)]
    near = [ring(1), ring(-1), ring(2), ring(-2)]

    barrier = pltpu.get_barrier_semaphore()
    partners = near + to_z + to_y + to_x + to_shot
    for d in partners:
        pl.semaphore_signal(barrier, inc=1, device_id=d, device_id_type=MESH)

    loads = [
        pltpu.make_async_copy(a, b, load_sem.at[i])
        for i, (a, b) in enumerate(
            (
                (cells_in, cells), (weights_in, weights), (p0_in, P0), (v_in, V), (pm_in, PM),
                (cell_in, cell), (wave_in, wave), (a0_in, A0), (am_in, AM), (obs_in, obs),
            )
        )
    ]
    for c in loads:
        c.start()

    sent = []

    def send(src, dst, to):
        i = len(sent)
        c = pltpu.make_async_remote_copy(
            src_ref=src, dst_ref=dst, send_sem=send_sem.at[i], recv_sem=recv_sem.at[i], device_id=to, device_id_type=MESH
        )
        c.start()
        sent.append(c)
        return c

    lo4, hi4 = pl.ds(0, 4), pl.ds(rows - 4, 4)

    dz[...] = band(iota((2 * nz, nz), 0) % nz, iota((2 * nz, nz), 1))
    dy[...] = band(iota((ny, 2 * ny), 0), iota((ny, 2 * ny), 1) % ny)

    loads[0].wait()
    loads[1].wait()
    at = cells[...]
    at_z = at[0:1] & (nz - 1)
    at_y = (at[0:1] // nz) & (ny - 1)
    hot = jnp.where(iota((nz, traces), 0) == at_z, 1.0, 0.0)
    ozT[pl.ds(0, nz)] = hot.astype(BF16)
    ozT[pl.ds(nz, nz)] = hot.astype(BF16)
    hot_t = jnp.transpose(hot).astype(BF16)
    oz[pl.ds(0, traces)] = hot_t
    oz[pl.ds(traces, traces)] = hot_t
    oyT[...] = jnp.where(iota((ny, traces), 0) == at_y, 1.0, 0.0).astype(BF16)
    at_x = at // (nz * ny) - s * rows + 4
    w = weights[...]
    acc = jnp.zeros((rows + 8, traces), F32)
    row_id = iota((rows + 8, traces), 0)
    for k in range(at.shape[0]):
        acc = acc + jnp.where(at_x[k : k + 1] == row_id, w[k : k + 1], 0.0)
    wx[...] = acc

    left_edge = jnp.where(s > 0, 1.0, 0.0).astype(F32)
    right_edge = jnp.where(s < n_space - 1, 1.0, 0.0).astype(F32)

    for k in (2, 3, 4, 5, 6):
        loads[k].wait()
    place = cell[...] - s * (rows * ny * nz)
    flat = iota((ny, nz), 0) * nz + iota((ny, nz), 1)
    spots = [jnp.where(flat + i * (ny * nz) == place, 1.0, 0.0) for i in range(rows)]
    p0 = P0[...]
    lap = lap_inside(p0, dz[...], dy[...])
    for i in range(rows):
        LAP0[i] = lap[i]
        P1[i] = 2.0 * p0[i] - PM[i] + V[i] * (lap[i] + spots[i] * wave[0:1, 0:1])
    loads[7].wait()
    loads[8].wait()
    a0 = A0[...]
    lap = lap_inside(a0, dz[...], dy[...])
    for i in range(rows):
        A1[4 + i] = 2.0 * a0[i] - AM[i] + V[i] * lap[i]

    loads[9].wait()
    lane0, row0 = (s * 8) % 128, (s * 8) // 128
    obs_wide[...] = jnp.zeros(obs_wide.shape, F32)
    obs_wide[pl.ds(0, 2), pl.ds(0, 8)] = obs[...]
    rolled = pltpu.roll(obs_wide[...], lane0, 1)
    which = iota((8, 128), 0)
    sums[0] = jnp.where(which == row0, rolled[0:1], 0.0) + jnp.where(which == blocks + row0, rolled[1:2], 0.0)

    pl.semaphore_wait(barrier, len(partners))

    def exchange(field, low, high):
        a = send(low, halo.at[field, 1], ring(-1))
        b = send(high, halo.at[field, 0], ring(1))
        return b, a

    got_p0 = exchange(0, p0_in.at[lo4], p0_in.at[hi4])
    got_a0 = exchange(1, a0_in.at[lo4], a0_in.at[hi4])
    obs_y = [send(sums.at[0], sums_y.at[0, k], d) for k, d in enumerate(to_y)]
    got_v = exchange(2, v_in.at[lo4], v_in.at[hi4])

    got_p0[0].wait_recv()
    hl = halo[0, 0]
    for i in range(4):
        add = from_left(hl, i, left_edge)
        LAP0[i] += add
        P1[i] += V[i] * add
    p1_left = send(P1.at[lo4], halo.at[3, 1], ring(-1))
    got_p0[1].wait_recv()
    hr = halo[0, 1]
    for i in range(4):
        add = from_right(hr, i, right_edge)
        LAP0[rows - 4 + i] += add
        P1[rows - 4 + i] += V[rows - 4 + i] * add
    p1_right = send(P1.at[hi4], halo.at[3, 0], ring(1))

    def sample(f, k):
        hi, lo = split(f)
        g = dot(jnp.concatenate([hi.reshape(rows * ny, nz), lo.reshape(rows * ny, nz)], axis=1), ozT[...])
        acc = wx[4:5] * g[0:ny]
        for i in range(1, rows):
            acc = acc + wx[4 + i : 5 + i] * g[i * ny : (i + 1) * ny]
        line = jnp.sum(acc * oyT[...].astype(F32), axis=0, keepdims=True)
        part[k] = jnp.zeros((8, 128), F32)
        for b in range(blocks):
            part[k, pl.ds(k * blocks + b, 1), :] = line[:, b * 128 : (b + 1) * 128]
        return [send(part.at[k], part_in.at[k, i], d) for i, d in enumerate(near)]

    p1 = P1[...]
    got_part = [sample(p1, 0)]
    lap = lap_inside(p1, dz[...], dy[...])
    for i in range(rows):
        LAP1[i] = lap[i]
        P2[i] = 2.0 * p1[i] - P0[i] + V[i] * (lap[i] + spots[i] * wave[0:1, 1:2])

    got_a0[0].wait_recv()
    hl = halo[1, 0]
    for i in range(4):
        A1[4 + i] += V[i] * from_left(hl, i, left_edge)
    b1_left = send(A1.at[pl.ds(4, 4)], halo.at[4, 1], ring(-1))
    got_a0[1].wait_recv()
    hr = halo[1, 1]
    for i in range(4):
        A1[rows + i] += V[rows - 4 + i] * from_right(hr, i, right_edge)
    b1_right = send(A1.at[pl.ds(rows, 4)], halo.at[4, 0], ring(1))

    def gather(got, own, ref, slot, count):
        total = own
        for c in got:
            c.wait_recv()
        for k in range(count):
            total = total + ref[slot, k]
        return total

    sums[1] = gather(obs_y, sums[0], sums_y, 0, ny_ - 1)
    obs_z = [send(sums.at[1], sums_z.at[0, k], d) for k, d in enumerate(to_z)]

    p1_right.wait_recv()
    hl = halo[3, 0]
    for i in range(4):
        add = from_left(hl, i, left_edge)
        LAP1[i] += add
        P2[i] += V[i] * add
    p1_left.wait_recv()
    hr = halo[3, 1]
    for i in range(4):
        add = from_right(hr, i, right_edge)
        LAP1[rows - 4 + i] += add
        P2[rows - 4 + i] += V[rows - 4 + i] * add
    got_part.append(sample(P2[...], 1))
    outs = [pltpu.make_async_copy(P2, f_out, out_sem.at[0])]
    outs[0].start()
    sums[3] = part[0] + part[1]
    res_y = [send(sums.at[3], sums_y.at[1, k], d) for k, d in enumerate(to_y)]

    sums[2] = gather(obs_z, sums[1], sums_z, 0, nz_ - 1)
    obs_x = [send(sums.at[2], sums_x.at[0, k], d) for k, d in enumerate(to_x)]

    def inject(k, first, count):
        arow[k] = gather(got_part[k], part[k], part_in, k, 4) - observed
        line = jnp.concatenate([arow[k, pl.ds(k * blocks + b, 1), :] for b in range(blocks)], axis=1)
        hi, lo = split(wx[pl.ds(first, count)] * line)
        hot = oyT[...]
        lhs = jnp.concatenate(
            [jnp.concatenate([hot * hi[i : i + 1], hot * lo[i : i + 1]], axis=1) for i in range(count)], axis=0
        )
        return dot(lhs, oz[...])

    observed = gather(obs_x, sums[2], sums_x, 0, nx_ - 1)

    inj = inject(0, 4, rows)
    for i in range(rows):
        INJ0[i] = V[i] * inj[i * ny : (i + 1) * ny]
    got_v[0].wait_recv()
    got_v[1].wait_recv()
    b1_right.wait_recv()
    b1_left.wait_recv()
    b1_left.wait_send()
    b1_right.wait_send()
    inj = inject(1, 0, rows + 8)
    for i in range(4):
        A1[i] = halo[4, 0, i] * left_edge + halo[2, 0, i] * inj[i * ny : (i + 1) * ny]
        k = rows + 4 + i
        A1[k] = halo[4, 1, i] * right_edge + halo[2, 1, i] * inj[k * ny : (k + 1) * ny]
    for i in range(rows):
        k = 4 + i
        A1[k] += V[i] * inj[k * ny : (k + 1) * ny]
    a1 = A1[...]
    lap = lap_inside(a1[4 : 4 + rows], dz[...], dy[...])
    scale = 1.0 / n_shot
    for i in range(rows):
        lp = lap[i]
        if i < 4:
            lp = lp + from_left(a1[0:4], i, 1.0)
        if i >= rows - 4:
            lp = lp + from_right(a1[rows + 4 :], i - rows + 4, 1.0)
        a2 = 2.0 * a1[4 + i] - A0[i] + V[i] * lp + INJ0[i]
        A2[i] = a2
        terms[i] = (a1[4 + i] * LAP1[i] + a2 * LAP0[i]) * scale
    got_g = [
        send(terms.at[:, pl.ds(pl.multiple_of(d[0] * 8, 8), 8)], gin.at[k], d) for k, d in enumerate(to_shot)
    ]
    outs.append(pltpu.make_async_copy(A2, a_out, out_sem.at[1]))
    outs[1].start()

    sums[4] = gather(res_y, sums[3], sums_y, 1, ny_ - 1)
    res_z = [send(sums.at[4], sums_z.at[1, k], d) for k, d in enumerate(to_z)]
    sums[5] = gather(res_z, sums[4], sums_z, 1, nz_ - 1)
    res_x = [send(sums.at[5], sums_x.at[1, k], d) for k, d in enumerate(to_x)]

    total = terms[:, pl.ds(pl.multiple_of(h * 8, 8), 8)]
    for c in got_g:
        c.wait_recv()
    for k in range(n_shot - 1):
        total = total + gin[k]
    grad[...] = total
    outs.append(pltpu.make_async_copy(grad, g_out, out_sem.at[2]))
    outs[2].start()

    every = gather(res_x, sums[5], sums_x, 1, nx_ - 1)
    picked = jnp.concatenate(
        [
            jnp.sum(jnp.where(which == k * blocks + row0, every, 0.0), axis=0, keepdims=True)
            for k in range(2)
        ],
        axis=0,
    )
    obs_wide[pl.ds(0, 2)] = picked
    rolled = pltpu.roll(obs_wide[...], (128 - lane0) % 128, 1)
    res[...] = rolled[0:2, 0:8] - obs[...]
    outs.append(pltpu.make_async_copy(res, r_out, out_sem.at[3]))
    outs[3].start()

    for c in sent:
        if c is not b1_left and c is not b1_right:
            c.wait_send()
    for c in outs:
        c.wait()


def solution(mesh):
    n_shot, n_space = mesh.shape["shot"], mesh.shape["space"]
    sizes = (n_shot, n_space, 4, 2, n_space // 8)

    def per_device(v, pm, p0, am, a0, cell, wave, cells, weights, obs):
        rows, ny, nz = v.shape
        traces = weights.shape[1]
        slab = (rows, ny, nz)
        anywhere = pl.BlockSpec(memory_space=pl.ANY)
        vm = lambda *shape: pltpu.VMEM(shape, F32)
        count = 5 * 2 + 2 * 4 + 2 * (sizes[2] + sizes[3] + sizes[4] - 3) + n_shot - 1
        f, a, r, g = pl.pallas_call(
            functools.partial(kernel, sizes),
            out_shape=(
                jax.ShapeDtypeStruct(slab, F32),
                jax.ShapeDtypeStruct(slab, F32),
                jax.ShapeDtypeStruct((2, 8), F32),
                jax.ShapeDtypeStruct((rows, ny // n_shot, nz), F32),
            ),
            in_specs=[anywhere] * 10,
            out_specs=[anywhere] * 4,
            scratch_shapes=[vm(*slab)] * 9
            + [vm(rows + 8, ny, nz), vm(*slab), vm(*slab), vm(*slab), vm(rows, ny // n_shot, nz)]
            + [
                pltpu.VMEM((1, 1), jnp.int32),
                vm(1, 2),
                pltpu.VMEM((8, traces), jnp.int32),
                vm(8, traces),
                vm(2, 8),
                vm(8, 128),
                vm(2, 8),
                vm(5, 2, 4, ny, nz),
                pltpu.VMEM((2 * nz, traces), BF16),
                pltpu.VMEM((2 * traces, nz), BF16),
                pltpu.VMEM((ny, traces), BF16),
                vm(rows + 8, traces),
                pltpu.VMEM((2 * nz, nz), BF16),
                pltpu.VMEM((ny, 2 * ny), BF16),
                vm(2, 8, 128),
                vm(2, 4, 8, 128),
                vm(2, 8, 128),
                vm(6, 8, 128),
                vm(2, sizes[4] - 1, 8, 128),
                vm(2, sizes[3] - 1, 8, 128),
                vm(2, sizes[2] - 1, 8, 128),
                vm(n_shot - 1, rows, ny // n_shot, nz),
                pltpu.SemaphoreType.DMA((10,)),
                pltpu.SemaphoreType.DMA((4,)),
                pltpu.SemaphoreType.DMA((count,)),
                pltpu.SemaphoreType.DMA((count,)),
            ],
            compiler_params=pltpu.CompilerParams(collective_id=0, has_side_effects=True, vmem_limit_bytes=40 << 20),
            cost_estimate=pl.CostEstimate(flops=10**9, bytes_accessed=2 << 20, transcendentals=0),
            name="two_steps",
        )(
            v, pm[0], p0[0], am[0], a0[0], cell.reshape(1, 1), wave,
            jnp.transpose(cells[0]), jnp.transpose(weights[0]), obs[0],
        )
        return f[None], a[None], r[None], g

    field = P("shot", "space", None, None)
    return jax.shard_map(
        per_device,
        mesh=mesh,
        in_specs=(
            P("space", None, None), field, field, field, field,
            P("shot"), P("shot", None), P("shot", None, None), P("shot", None, None), P("shot", None, "space"),
        ),
        out_specs=(field, field, P("shot", None, "space"), P("space", "shot", None)),
        check_vma=False,
    )
```

```python
import functools

import jax
import jax.numpy as jnp
from jax import lax
from jax.experimental import pallas as pl
from jax.experimental.pallas import tpu as pltpu
from jax.sharding import PartitionSpec as P

MESH = pl.DeviceIdType.MESH
F32, BF16 = jnp.float32, jnp.bfloat16
coeffs = (-205.0 / 72.0, 8.0 / 5.0, -1.0 / 5.0, 8.0 / 315.0, -1.0 / 560.0)
whole = (8064.0, -1008.0, 128.0, -9.0)


def split(f):
    hi = f.astype(BF16)
    return hi, (f - hi.astype(F32)).astype(BF16)


def dot(a, b):
    return jnp.dot(a, b, preferred_element_type=F32)


def band(i, j):
    d = jnp.abs(i - j)
    m = jnp.zeros(d.shape, F32)
    for k, c in enumerate(whole):
        m = jnp.where(d == k + 1, c, m)
    return m.astype(BF16)


def iota(shape, dim):
    return lax.broadcasted_iota(jnp.int32, shape, dim)


def lap_inside(f, dz, dy):
    rows, ny, nz = f.shape
    hi, lo = split(f)
    zz = dot(jnp.concatenate([hi.reshape(rows * ny, nz), lo.reshape(rows * ny, nz)], axis=1), dz)
    yy = dot(dy, jnp.concatenate([jnp.concatenate([hi[x], lo[x]], axis=0) for x in range(rows)], axis=1))
    out = []
    for x in range(rows):
        r = 3.0 * coeffs[0] * f[x] + (zz[x * ny : (x + 1) * ny] + yy[:, x * nz : (x + 1) * nz]) * (1.0 / 5040.0)
        for j in range(1, 5):
            terms = [f[k] for k in (x - j, x + j) if 0 <= k < rows]
            if terms:
                r = r + coeffs[j] * functools.reduce(jnp.add, terms)
        out.append(r)
    return out


def from_left(h, i, edge):
    return functools.reduce(jnp.add, [(coeffs[j] * edge) * h[4 + i - j] for j in range(i + 1, 5)])


def from_right(h, i, edge):
    return functools.reduce(jnp.add, [(coeffs[j] * edge) * h[i + j - 4] for j in range(4 - i, 5)])


def kernel(
    sizes,
    v_in, pm_in, p0_in, am_in, a0_in, cell_in, wave_in, cells_in, weights_in, obs_in,
    f_out, a_out, r_out, g_out,
    V, PM, P0, AM, A0, LAP0, P1, LAP1, A1, INJ0, terms, P2, A2, res, grad,
    cell, wave, cells, weights, obs, obs_wide,
    halo, ozT, oz, oyT, wx, dz, dy,
    part, part_in, arow, sums, sums_y, sums_z, sums_x, gin,
    load_sem, out_sem, send_sem, recv_sem,
):
    n_shot, n_space, nx_, nz_, ny_ = sizes
    rows, ny, nz = V.shape
    traces = weights.shape[1]
    blocks = traces // 128
    h = lax.axis_index("shot")
    s = lax.axis_index("space")
    x, zh, y = s % nx_, (s // nx_) % nz_, s // (nx_ * nz_)

    def ring(k):
        return (h, (s + k + n_space) % n_space)

    def slab(x, zh, y):
        return (h, (y * nz_ + zh) * nx_ + x)

    to_y = [slab(x, zh, (y + k) % ny_) for k in range(1, ny_)]
    to_z = [slab(x, (zh + k) % nz_, y) for k in range(1, nz_)]
    to_x = [slab((x + k) % nx_, zh, y) for k in range(1, nx_)]
    to_shot = [((h + k) % n_shot, s) for k in range(1, n_shot)]
    near = [ring(1), ring(-1), ring(2), ring(-2)]

    barrier = pltpu.get_barrier_semaphore()
    partners = near + to_z + to_y + to_x + to_shot
    for d in partners:
        pl.semaphore_signal(barrier, inc=1, device_id=d, device_id_type=MESH)

    loads = [
        pltpu.make_async_copy(a, b, load_sem.at[i])
        for i, (a, b) in enumerate(
            (
                (cells_in, cells), (weights_in, weights), (p0_in, P0), (v_in, V), (pm_in, PM),
                (cell_in, cell), (wave_in, wave), (a0_in, A0), (am_in, AM), (obs_in, obs),
            )
        )
    ]
    for c in loads:
        c.start()

    sent = []

    def send(src, dst, to):
        i = len(sent)
        c = pltpu.make_async_remote_copy(
            src_ref=src, dst_ref=dst, send_sem=send_sem.at[i], recv_sem=recv_sem.at[i], device_id=to, device_id_type=MESH
        )
        c.start()
        sent.append(c)
        return c

    lo4, hi4 = pl.ds(0, 4), pl.ds(rows - 4, 4)

    dz[...] = band(iota((2 * nz, nz), 0) % nz, iota((2 * nz, nz), 1))
    dy[...] = band(iota((ny, 2 * ny), 0), iota((ny, 2 * ny), 1) % ny)

    loads[0].wait()
    loads[1].wait()
    at = cells[...]
    at_z = at[0:1] & (nz - 1)
    at_y = (at[0:1] // nz) & (ny - 1)
    hot = jnp.where(iota((nz, traces), 0) == at_z, 1.0, 0.0)
    ozT[pl.ds(0, nz)] = hot.astype(BF16)
    ozT[pl.ds(nz, nz)] = hot.astype(BF16)
    hot_t = jnp.transpose(hot).astype(BF16)
    oz[pl.ds(0, traces)] = hot_t
    oz[pl.ds(traces, traces)] = hot_t
    oyT[...] = jnp.where(iota((ny, traces), 0) == at_y, 1.0, 0.0).astype(BF16)
    at_x = at // (nz * ny) - s * rows + 4
    w = weights[...]
    acc = jnp.zeros((rows + 8, traces), F32)
    row_id = iota((rows + 8, traces), 0)
    for k in range(at.shape[0]):
        acc = acc + jnp.where(at_x[k : k + 1] == row_id, w[k : k + 1], 0.0)
    wx[...] = acc

    left_edge = jnp.where(s > 0, 1.0, 0.0).astype(F32)
    right_edge = jnp.where(s < n_space - 1, 1.0, 0.0).astype(F32)

    for k in (2, 3, 4, 5, 6):
        loads[k].wait()
    place = cell[...] - s * (rows * ny * nz)
    flat = iota((ny, nz), 0) * nz + iota((ny, nz), 1)
    spots = [jnp.where(flat + i * (ny * nz) == place, 1.0, 0.0) for i in range(rows)]
    p0 = P0[...]
    lap = lap_inside(p0, dz[...], dy[...])
    for i in range(rows):
        LAP0[i] = lap[i]
        P1[i] = 2.0 * p0[i] - PM[i] + V[i] * (lap[i] + spots[i] * wave[0:1, 0:1])
    loads[7].wait()
    loads[8].wait()
    a0 = A0[...]
    lap = lap_inside(a0, dz[...], dy[...])
    for i in range(rows):
        A1[4 + i] = 2.0 * a0[i] - AM[i] + V[i] * lap[i]

    loads[9].wait()
    lane0, row0 = (s * 8) % 128, (s * 8) // 128
    obs_wide[...] = jnp.zeros(obs_wide.shape, F32)
    obs_wide[pl.ds(0, 2), pl.ds(0, 8)] = obs[...]
    rolled = pltpu.roll(obs_wide[...], lane0, 1)
    which = iota((8, 128), 0)
    sums[0] = jnp.where(which == row0, rolled[0:1], 0.0) + jnp.where(which == blocks + row0, rolled[1:2], 0.0)

    pl.semaphore_wait(barrier, len(partners))

    def exchange(field, low, high):
        a = send(low, halo.at[field, 1], ring(-1))
        b = send(high, halo.at[field, 0], ring(1))
        return b, a

    got_p0 = exchange(0, p0_in.at[lo4], p0_in.at[hi4])
    got_a0 = exchange(1, a0_in.at[lo4], a0_in.at[hi4])
    obs_y = [send(sums.at[0], sums_y.at[0, k], d) for k, d in enumerate(to_y)]
    got_v = exchange(2, v_in.at[lo4], v_in.at[hi4])

    got_p0[0].wait_recv()
    hl = halo[0, 0]
    for i in range(4):
        add = from_left(hl, i, left_edge)
        LAP0[i] += add
        P1[i] += V[i] * add
    p1_left = send(P1.at[lo4], halo.at[3, 1], ring(-1))
    got_p0[1].wait_recv()
    hr = halo[0, 1]
    for i in range(4):
        add = from_right(hr, i, right_edge)
        LAP0[rows - 4 + i] += add
        P1[rows - 4 + i] += V[rows - 4 + i] * add
    p1_right = send(P1.at[hi4], halo.at[3, 0], ring(1))

    def sample(f, k):
        hi, lo = split(f)
        g = dot(jnp.concatenate([hi.reshape(rows * ny, nz), lo.reshape(rows * ny, nz)], axis=1), ozT[...])
        acc = wx[4:5] * g[0:ny]
        for i in range(1, rows):
            acc = acc + wx[4 + i : 5 + i] * g[i * ny : (i + 1) * ny]
        line = jnp.sum(acc * oyT[...].astype(F32), axis=0, keepdims=True)
        part[k] = jnp.zeros((8, 128), F32)
        for b in range(blocks):
            part[k, pl.ds(k * blocks + b, 1), :] = line[:, b * 128 : (b + 1) * 128]
        return [send(part.at[k], part_in.at[k, i], d) for i, d in enumerate(near)]

    p1 = P1[...]
    got_part = [sample(p1, 0)]
    lap = lap_inside(p1, dz[...], dy[...])
    for i in range(rows):
        LAP1[i] = lap[i]
        P2[i] = 2.0 * p1[i] - P0[i] + V[i] * (lap[i] + spots[i] * wave[0:1, 1:2])

    got_a0[0].wait_recv()
    hl = halo[1, 0]
    for i in range(4):
        A1[4 + i] += V[i] * from_left(hl, i, left_edge)
    b1_left = send(A1.at[pl.ds(4, 4)], halo.at[4, 1], ring(-1))
    got_a0[1].wait_recv()
    hr = halo[1, 1]
    for i in range(4):
        A1[rows + i] += V[rows - 4 + i] * from_right(hr, i, right_edge)
    b1_right = send(A1.at[pl.ds(rows, 4)], halo.at[4, 0], ring(1))

    def gather(got, own, ref, slot, count):
        total = own
        for c in got:
            c.wait_recv()
        for k in range(count):
            total = total + ref[slot, k]
        return total

    sums[1] = gather(obs_y, sums[0], sums_y, 0, ny_ - 1)
    obs_z = [send(sums.at[1], sums_z.at[0, k], d) for k, d in enumerate(to_z)]

    p1_right.wait_recv()
    hl = halo[3, 0]
    for i in range(4):
        add = from_left(hl, i, left_edge)
        LAP1[i] += add
        P2[i] += V[i] * add
    p1_left.wait_recv()
    hr = halo[3, 1]
    for i in range(4):
        add = from_right(hr, i, right_edge)
        LAP1[rows - 4 + i] += add
        P2[rows - 4 + i] += V[rows - 4 + i] * add
    got_part.append(sample(P2[...], 1))
    outs = [pltpu.make_async_copy(P2, f_out, out_sem.at[0])]
    outs[0].start()
    sums[3] = part[0] + part[1]
    res_y = [send(sums.at[3], sums_y.at[1, k], d) for k, d in enumerate(to_y)]

    sums[2] = gather(obs_z, sums[1], sums_z, 0, nz_ - 1)
    obs_x = [send(sums.at[2], sums_x.at[0, k], d) for k, d in enumerate(to_x)]

    def inject(k, first, count):
        arow[k] = gather(got_part[k], part[k], part_in, k, 4) - observed
        line = jnp.concatenate([arow[k, pl.ds(k * blocks + b, 1), :] for b in range(blocks)], axis=1)
        hi, lo = split(wx[pl.ds(first, count)] * line)
        hot = oyT[...]
        lhs = jnp.concatenate(
            [jnp.concatenate([hot * hi[i : i + 1], hot * lo[i : i + 1]], axis=1) for i in range(count)], axis=0
        )
        return dot(lhs, oz[...])

    observed = gather(obs_x, sums[2], sums_x, 0, nx_ - 1)

    inj = inject(0, 4, rows)
    for i in range(rows):
        INJ0[i] = V[i] * inj[i * ny : (i + 1) * ny]
    got_v[0].wait_recv()
    got_v[1].wait_recv()
    b1_right.wait_recv()
    b1_left.wait_recv()
    b1_left.wait_send()
    b1_right.wait_send()
    sums[4] = gather(res_y, sums[3], sums_y, 1, ny_ - 1)
    res_z = [send(sums.at[4], sums_z.at[1, k], d) for k, d in enumerate(to_z)]
    inj = inject(1, 0, rows + 8)
    for i in range(4):
        A1[i] = halo[4, 0, i] * left_edge + halo[2, 0, i] * inj[i * ny : (i + 1) * ny]
        k = rows + 4 + i
        A1[k] = halo[4, 1, i] * right_edge + halo[2, 1, i] * inj[k * ny : (k + 1) * ny]
    for i in range(rows):
        k = 4 + i
        A1[k] += V[i] * inj[k * ny : (k + 1) * ny]
    a1 = A1[...]
    lap = lap_inside(a1[4 : 4 + rows], dz[...], dy[...])
    scale = 1.0 / n_shot
    for i in range(rows):
        lp = lap[i]
        if i < 4:
            lp = lp + from_left(a1[0:4], i, 1.0)
        if i >= rows - 4:
            lp = lp + from_right(a1[rows + 4 :], i - rows + 4, 1.0)
        a2 = 2.0 * a1[4 + i] - A0[i] + V[i] * lp + INJ0[i]
        A2[i] = a2
        terms[i] = (a1[4 + i] * LAP1[i] + a2 * LAP0[i]) * scale
    got_g = [
        send(terms.at[:, pl.ds(pl.multiple_of(d[0] * 8, 8), 8)], gin.at[k], d) for k, d in enumerate(to_shot)
    ]

    sums[5] = gather(res_z, sums[4], sums_z, 1, nz_ - 1)
    res_x = [send(sums.at[5], sums_x.at[1, k], d) for k, d in enumerate(to_x)]

    outs.append(pltpu.make_async_copy(A2, a_out, out_sem.at[1]))
    outs[1].start()
    total = terms[:, pl.ds(pl.multiple_of(h * 8, 8), 8)]
    for c in got_g:
        c.wait_recv()
    for k in range(n_shot - 1):
        total = total + gin[k]
    grad[...] = total
    outs.append(pltpu.make_async_copy(grad, g_out, out_sem.at[2]))
    outs[2].start()

    every = gather(res_x, sums[5], sums_x, 1, nx_ - 1)
    picked = jnp.concatenate(
        [
            jnp.sum(jnp.where(which == k * blocks + row0, every, 0.0), axis=0, keepdims=True)
            for k in range(2)
        ],
        axis=0,
    )
    obs_wide[pl.ds(0, 2)] = picked
    rolled = pltpu.roll(obs_wide[...], (128 - lane0) % 128, 1)
    res[...] = rolled[0:2, 0:8] - obs[...]
    outs.append(pltpu.make_async_copy(res, r_out, out_sem.at[3]))
    outs[3].start()

    for c in sent:
        if c is not b1_left and c is not b1_right:
            c.wait_send()
    for c in outs:
        c.wait()


def store(*refs):
    given, given_back, held, sems = refs[:4], refs[4:8], refs[8:12], refs[12]
    loads = [pltpu.make_async_copy(a, b, sems.at[0, i]) for i, (a, b) in enumerate(zip(given, held))]
    stores = [pltpu.make_async_copy(a, b, sems.at[1, i]) for i, (a, b) in enumerate(zip(held, given_back))]
    for c in loads:
        c.start()
    for c, d in zip(loads, stores):
        c.wait()
        d.start()
    for c in stores:
        c.wait()


def solution(mesh):
    n_shot, n_space = mesh.shape["shot"], mesh.shape["space"]
    sizes = (n_shot, n_space, 4, 2, n_space // 8)

    def per_device(v, pm, p0, am, a0, cell, wave, cells, weights, obs):
        rows, ny, nz = v.shape
        traces = weights.shape[1]
        slab = (rows, ny, nz)
        hbm = pl.BlockSpec(memory_space=pltpu.HBM)
        vm = lambda *shape: pltpu.VMEM(shape, F32)
        count = 5 * 2 + 2 * 4 + 2 * (sizes[2] + sizes[3] + sizes[4] - 3) + n_shot - 1
        results = (
                jax.ShapeDtypeStruct(slab, F32),
                jax.ShapeDtypeStruct(slab, F32),
                jax.ShapeDtypeStruct((2, 8), F32),
                jax.ShapeDtypeStruct((rows, ny // n_shot, nz), F32),
            )
        out = pl.pallas_call(
            functools.partial(kernel, sizes),
            out_shape=results,
            in_specs=[hbm] * 10,
            out_specs=[hbm] * 4,
            scratch_shapes=[vm(*slab)] * 8
            + [vm(rows + 8, ny, nz), vm(*slab), vm(*slab), vm(*slab), vm(*slab), vm(2, 8), vm(rows, ny // n_shot, nz)]
            + [
                pltpu.VMEM((1, 1), jnp.int32),
                vm(1, 2),
                pltpu.VMEM((8, traces), jnp.int32),
                vm(8, traces),
                vm(2, 8),
                vm(8, 128),
                vm(5, 2, 4, ny, nz),
                pltpu.VMEM((2 * nz, traces), BF16),
                pltpu.VMEM((2 * traces, nz), BF16),
                pltpu.VMEM((ny, traces), BF16),
                vm(rows + 8, traces),
                pltpu.VMEM((2 * nz, nz), BF16),
                pltpu.VMEM((ny, 2 * ny), BF16),
                vm(2, 8, 128),
                vm(2, 4, 8, 128),
                vm(2, 8, 128),
                vm(6, 8, 128),
                vm(2, sizes[4] - 1, 8, 128),
                vm(2, sizes[3] - 1, 8, 128),
                vm(2, sizes[2] - 1, 8, 128),
                vm(n_shot - 1, rows, ny // n_shot, nz),
                pltpu.SemaphoreType.DMA((10,)),
                pltpu.SemaphoreType.DMA((4,)),
                pltpu.SemaphoreType.DMA((count,)),
                pltpu.SemaphoreType.DMA((count,)),
            ],
            compiler_params=pltpu.CompilerParams(collective_id=0, has_side_effects=True, vmem_limit_bytes=56 << 20),
            cost_estimate=pl.CostEstimate(flops=10**9, bytes_accessed=2 << 20, transcendentals=0),
            name="two_steps",
        )(
            v, pm[0], p0[0], am[0], a0[0], cell.reshape(1, 1), wave,
            jnp.transpose(cells[0]), jnp.transpose(weights[0]), obs[0],
        )
        f, a, r, g = pl.pallas_call(
            store,
            out_shape=results,
            in_specs=[hbm] * 4,
            out_specs=[hbm] * 4,
            scratch_shapes=[vm(*r.shape) for r in results] + [pltpu.SemaphoreType.DMA((2, 4))],
            name="store",
        )(*out)
        return f[None], a[None], r[None], g

    field = P("shot", "space", None, None)
    return jax.shard_map(
        per_device,
        mesh=mesh,
        in_specs=(
            P("space", None, None), field, field, field, field,
            P("shot"), P("shot", None), P("shot", None, None), P("shot", None, None), P("shot", None, "space"),
        ),
        out_specs=(field, field, P("shot", None, "space"), P("space", "shot", None)),
        check_vma=False,
    )
```

```python
import functools

import jax
import jax.numpy as jnp
from jax import lax
from jax.experimental import pallas as pl
from jax.experimental.pallas import tpu as pltpu
from jax.sharding import PartitionSpec as P

MESH = pl.DeviceIdType.MESH
F32, BF16 = jnp.float32, jnp.bfloat16
coeffs = (-205.0 / 72.0, 8.0 / 5.0, -1.0 / 5.0, 8.0 / 315.0, -1.0 / 560.0)
whole = (8064.0, -1008.0, 128.0, -9.0)


CHUNKS = 1


def split(f):
    hi = f.astype(BF16)
    return hi, (f - hi.astype(F32)).astype(BF16)


def dot(a, b):
    return jnp.dot(a, b, preferred_element_type=F32)


def band(i, j):
    d = jnp.abs(i - j)
    m = jnp.zeros(d.shape, F32)
    for k, c in enumerate(whole):
        m = jnp.where(d == k + 1, c, m)
    return m.astype(BF16)


def iota(shape, dim):
    return lax.broadcasted_iota(jnp.int32, shape, dim)


def lap_inside(f, dz, dy):
    rows, ny, nz = f.shape
    hi, lo = split(f)
    zz = dot(jnp.concatenate([hi.reshape(rows * ny, nz), lo.reshape(rows * ny, nz)], axis=1), dz)
    yy = dot(dy, jnp.concatenate([jnp.concatenate([hi[x], lo[x]], axis=0) for x in range(rows)], axis=1))
    out = []
    for x in range(rows):
        r = 3.0 * coeffs[0] * f[x] + (zz[x * ny : (x + 1) * ny] + yy[:, x * nz : (x + 1) * nz]) * (1.0 / 5040.0)
        for j in range(1, 5):
            terms = [f[k] for k in (x - j, x + j) if 0 <= k < rows]
            if terms:
                r = r + coeffs[j] * functools.reduce(jnp.add, terms)
        out.append(r)
    return out


def from_left(h, i, edge):
    return functools.reduce(jnp.add, [(coeffs[j] * edge) * h[4 + i - j] for j in range(i + 1, 5)])


def from_right(h, i, edge):
    return functools.reduce(jnp.add, [(coeffs[j] * edge) * h[i + j - 4] for j in range(4 - i, 5)])


def kernel(
    sizes,
    v_in, pm_in, p0_in, am_in, a0_in, cell_in, wave_in, cells_in, weights_in, obs_in,
    f_out, a_out, r_out, g_out,
    V, PM, P0, AM, A0, LAP0, P1, LAP1, A1, terms, P2, A2, res, grad,
    cell, wave, cells, weights, obs, obs_wide,
    halo, outer, ozT, oz, oyT, wx, wv, vs, vs_in, dz, dy,
    part, part_in, arow, sums, sums_y, sums_z, sums_x, gin,
    load_sem, out_sem, send_sem, recv_sem,
):
    n_shot, n_space, nx_, nz_, ny_ = sizes
    rows, ny, nz = V.shape
    traces = weights.shape[1]
    blocks = traces // 128
    h = lax.axis_index("shot")
    s = lax.axis_index("space")
    x, zh, y = s % nx_, (s // nx_) % nz_, s // (nx_ * nz_)

    def ring(k):
        return (h, (s + k + n_space) % n_space)

    def slab(x, zh, y):
        return (h, (y * nz_ + zh) * nx_ + x)

    to_y = [slab(x, zh, (y + k) % ny_) for k in range(1, ny_)]
    to_z = [slab(x, (zh + k) % nz_, y) for k in range(1, nz_)]
    to_x = [slab((x + k) % nx_, zh, y) for k in range(1, nx_)]
    to_shot = [((h + k) % n_shot, s) for k in range(1, n_shot)]
    near = [ring(1), ring(-1), ring(2), ring(-2)]

    barrier = pltpu.get_barrier_semaphore()
    partners = near + to_z + to_y + to_x + to_shot
    for d in partners:
        pl.semaphore_signal(barrier, inc=1, device_id=d, device_id_type=MESH)

    loads = [
        pltpu.make_async_copy(a, b, load_sem.at[i])
        for i, (a, b) in enumerate(
            (
                (cells_in, cells), (weights_in, weights), (p0_in, P0), (v_in, V), (pm_in, PM),
                (cell_in, cell), (wave_in, wave), (a0_in, A0), (am_in, AM), (obs_in, obs),
            )
        )
    ]
    for c in loads:
        c.start()

    sent = []

    def send(src, dst, to):
        i = len(sent)
        c = pltpu.make_async_remote_copy(
            src_ref=src, dst_ref=dst, send_sem=send_sem.at[i], recv_sem=recv_sem.at[i], device_id=to, device_id_type=MESH
        )
        c.start()
        sent.append(c)
        return c

    lo4, hi4 = pl.ds(0, 4), pl.ds(rows - 4, 4)

    dz[...] = band(iota((2 * nz, nz), 0) % nz, iota((2 * nz, nz), 1))
    dy[...] = band(iota((ny, 2 * ny), 0), iota((ny, 2 * ny), 1) % ny)

    loads[0].wait()
    loads[1].wait()
    at = cells[...]
    at_z = at[0:1] & (nz - 1)
    at_y = (at[0:1] // nz) & (ny - 1)
    hot = jnp.where(iota((nz, traces), 0) == at_z, 1.0, 0.0)
    ozT[pl.ds(0, nz)] = hot.astype(BF16)
    ozT[pl.ds(nz, nz)] = hot.astype(BF16)
    hot_t = jnp.transpose(hot).astype(BF16)
    oz[pl.ds(0, traces)] = hot_t
    oz[pl.ds(traces, traces)] = hot_t
    oyT[...] = jnp.where(iota((ny, traces), 0) == at_y, 1.0, 0.0).astype(BF16)
    at_x = at // (nz * ny) - s * rows + 4
    w = weights[...]
    acc = jnp.zeros((rows + 8, traces), F32)
    row_id = iota((rows + 8, traces), 0)
    for k in range(at.shape[0]):
        acc = acc + jnp.where(at_x[k : k + 1] == row_id, w[k : k + 1], 0.0)
    wx[...] = acc

    left_edge = jnp.where(s > 0, 1.0, 0.0).astype(F32)
    right_edge = jnp.where(s < n_space - 1, 1.0, 0.0).astype(F32)

    def at_traces(f):
        hi, lo = split(f)
        g = dot(jnp.concatenate([hi.reshape(rows * ny, nz), lo.reshape(rows * ny, nz)], axis=1), ozT[...])
        return [g[i * ny : (i + 1) * ny] for i in range(rows)]

    def over_y(g):
        return jnp.sum(g * oyT[...].astype(F32), axis=0, keepdims=True)

    for k in (2, 3, 4, 5, 6):
        loads[k].wait()
    place = cell[...] - s * (rows * ny * nz)
    flat = iota((ny, nz), 0) * nz + iota((ny, nz), 1)
    spots = [jnp.where(flat + i * (ny * nz) == place, 1.0, 0.0) for i in range(rows)]
    p0 = P0[...]
    lap = lap_inside(p0, dz[...], dy[...])
    for i in range(rows):
        LAP0[i] = lap[i]
        P1[i] = 2.0 * p0[i] - PM[i] + V[i] * (lap[i] + spots[i] * wave[0:1, 0:1])
    loads[7].wait()
    loads[8].wait()
    a0 = A0[...]
    lap = lap_inside(a0, dz[...], dy[...])
    for i in range(rows):
        A1[i] = 2.0 * a0[i] - AM[i] + V[i] * lap[i]

    for i, g in enumerate(at_traces(V[...])):
        vs[i // 4, pl.ds(i % 4, 1)] = over_y(g)

    loads[9].wait()
    lane0, row0 = (s * 8) % 128, (s * 8) // 128
    obs_wide[...] = jnp.zeros(obs_wide.shape, F32)
    obs_wide[pl.ds(0, 2), pl.ds(0, 8)] = obs[...]
    rolled = pltpu.roll(obs_wide[...], lane0, 1)
    which = iota((8, 128), 0)
    sums[0] = jnp.where(which == row0, rolled[0:1], 0.0) + jnp.where(which == blocks + row0, rolled[1:2], 0.0)

    pl.semaphore_wait(barrier, len(partners))

    wide = ny // CHUNKS
    parts = [pl.ds(c * wide, wide) for c in range(CHUNKS)]

    def exchange(field, low, high, c):
        a = send(low.at[:, parts[c]], halo.at[field, 1, :, parts[c]], ring(-1))
        b = send(high.at[:, parts[c]], halo.at[field, 0, :, parts[c]], ring(1))
        return b, a

    got_p0 = [exchange(0, p0_in.at[lo4], p0_in.at[hi4], c) for c in range(CHUNKS)]
    obs_y = [send(sums.at[0], sums_y.at[0, k], d) for k, d in enumerate(to_y)]
    got_a0 = [exchange(1, a0_in.at[lo4], a0_in.at[hi4], c) for c in range(CHUNKS)]
    vs_right = send(vs.at[0], vs_in.at[1], ring(-1))
    vs_left = send(vs.at[1], vs_in.at[0], ring(1))

    def gather(got, own, ref, slot, count):
        total = own
        for c in got:
            c.wait_recv()
        for k in range(count):
            total = total + ref[slot, k]
        return total

    sums[1] = gather(obs_y, sums[0], sums_y, 0, ny_ - 1)
    obs_z = [send(sums.at[1], sums_z.at[0, k], d) for k, d in enumerate(to_z)]

    got_p1 = []
    for c, ys in enumerate(parts):
        got_p0[c][0].wait_recv()
        hl = halo[0, 0, :, ys]
        for i in range(4):
            add = from_left(hl, i, left_edge)
            LAP0[i, ys] += add
            P1[i, ys] += V[i, ys] * add
        got_p0[c][1].wait_recv()
        hr = halo[0, 1, :, ys]
        for i in range(4):
            k = rows - 4 + i
            add = from_right(hr, i, right_edge)
            LAP0[k, ys] += add
            P1[k, ys] += V[k, ys] * add
        got_p1.append(exchange(2, P1.at[lo4], P1.at[hi4], c))

    p1 = P1[...]
    lines = [over_y(g) for g in at_traces(p1)]
    lap = lap_inside(p1, dz[...], dy[...])
    for i in range(rows):
        LAP1[i] = lap[i]
        P2[i] = 2.0 * p1[i] - P0[i] + V[i] * (lap[i] + spots[i] * wave[0:1, 1:2])
    acc = functools.reduce(jnp.add, [wx[4 + i : 5 + i] * g for i, g in enumerate(at_traces(P2[...]))])
    second = over_y(acc)
    first = functools.reduce(jnp.add, [wx[4 + i : 5 + i] * lines[i] for i in range(rows)])
    vs_left.wait_recv()
    vs_right.wait_recv()
    wv[pl.ds(0, 4)] = wx[0:4] * vs_in[0]
    wv[pl.ds(4, 4)] = wx[4:8] * vs[0]
    wv[pl.ds(8, 4)] = wx[8:12] * vs[1]
    wv[pl.ds(12, 4)] = wx[12:16] * vs_in[1]
    for i in range(4):
        second = second + wv[i : i + 1] * from_right(lines[0:4], i, 1.0)
        second = second + wv[rows + 4 + i : rows + 5 + i] * from_left(lines[rows - 4 :], i, 1.0)
    for k, line in enumerate((first, second)):
        for b in range(blocks):
            part[pl.ds(k * blocks + b, 1), :] = line[:, b * 128 : (b + 1) * 128]
    got_part = [send(part, part_in.at[i], d) for i, d in enumerate(near)]
    res_y = [send(part, sums_y.at[1, k], d) for k, d in enumerate(to_y)]

    got_b1 = []
    for c, ys in enumerate(parts):
        got_a0[c][0].wait_recv()
        hl = halo[1, 0, :, ys]
        for i in range(4):
            A1[i, ys] += V[i, ys] * from_left(hl, i, left_edge)
        got_a0[c][1].wait_recv()
        hr = halo[1, 1, :, ys]
        for i in range(4):
            k = rows - 4 + i
            A1[k, ys] += V[k, ys] * from_right(hr, i, right_edge)
        got_b1.append(exchange(3, A1.at[lo4], A1.at[hi4], c))

    sums[2] = gather(obs_z, sums[1], sums_z, 0, nz_ - 1)
    obs_x = [send(sums.at[2], sums_x.at[0, k], d) for k, d in enumerate(to_x)]

    for c, ys in enumerate(parts):
        got_p1[c][0].wait_recv()
        hl = halo[2, 0, :, ys]
        for i in range(4):
            add = from_left(hl, i, left_edge)
            LAP1[i, ys] += add
            P2[i, ys] += V[i, ys] * add
        got_p1[c][1].wait_recv()
        hr = halo[2, 1, :, ys]
        for i in range(4):
            k = rows - 4 + i
            add = from_right(hr, i, right_edge)
            LAP1[k, ys] += add
            P2[k, ys] += V[k, ys] * add
    outs = [pltpu.make_async_copy(P2, f_out, out_sem.at[0])]
    outs[0].start()

    sums[4] = gather(res_y, part[...], sums_y, 1, ny_ - 1)
    res_z = [send(sums.at[4], sums_z.at[1, k], d) for k, d in enumerate(to_z)]

    observed = gather(obs_x, sums[2], sums_x, 0, nx_ - 1)
    for c in got_part:
        c.wait_recv()
    arow[...] = functools.reduce(jnp.add, [part_in[i] for i in range(4)]) + part[...] - observed

    def inject(k, first, count):
        line = jnp.concatenate([arow[pl.ds(k * blocks + b, 1), :] for b in range(blocks)], axis=1)
        hi, lo = split(wv[pl.ds(first, count)] * line)
        hot = oyT[...]
        lhs = jnp.concatenate(
            [jnp.concatenate([hot * hi[i : i + 1], hot * lo[i : i + 1]], axis=1) for i in range(count)], axis=0
        )
        inj = dot(lhs, oz[...])
        return [inj[i * ny : (i + 1) * ny] for i in range(count)]

    for pair in got_b1:
        for c in pair:
            c.wait_send()
    inj = inject(1, 0, rows + 8)
    for i in range(4):
        outer[0, i] = inj[i]
        outer[1, i] = inj[rows + 4 + i]
    for i in range(rows):
        A1[i] += inj[4 + i]
    a1 = A1[...]
    inj = inject(0, 4, rows)
    lap = lap_inside(a1, dz[...], dy[...])
    scale = 1.0 / n_shot
    for i in range(rows):
        a2 = 2.0 * a1[i] - A0[i] + V[i] * lap[i] + inj[i]
        A2[i] = a2
        terms[i] = (a1[i] * LAP1[i] + a2 * LAP0[i]) * scale
    for c, ys in enumerate(parts):
        got_b1[c][0].wait_recv()
        hl = halo[3, 0, :, ys] * left_edge + outer[0, :, ys]
        for i in range(4):
            add = V[i, ys] * from_left(hl, i, 1.0)
            A2[i, ys] += add
            terms[i, ys] += add * LAP0[i, ys] * scale
        got_b1[c][1].wait_recv()
        hr = halo[3, 1, :, ys] * right_edge + outer[1, :, ys]
        for i in range(4):
            k = rows - 4 + i
            add = V[k, ys] * from_right(hr, i, 1.0)
            A2[k, ys] += add
            terms[k, ys] += add * LAP0[k, ys] * scale
    got_g = [
        send(terms.at[:, pl.ds(pl.multiple_of(d[0] * 8, 8), 8)], gin.at[k], d) for k, d in enumerate(to_shot)
    ]
    outs.append(pltpu.make_async_copy(A2, a_out, out_sem.at[1]))
    outs[1].start()

    sums[5] = gather(res_z, sums[4], sums_z, 1, nz_ - 1)
    res_x = [send(sums.at[5], sums_x.at[1, k], d) for k, d in enumerate(to_x)]

    total = terms[:, pl.ds(pl.multiple_of(h * 8, 8), 8)]
    for c in got_g:
        c.wait_recv()
    for k in range(n_shot - 1):
        total = total + gin[k]
    grad[...] = total
    outs.append(pltpu.make_async_copy(grad, g_out, out_sem.at[2]))
    outs[2].start()

    every = gather(res_x, sums[5], sums_x, 1, nx_ - 1)
    picked = jnp.concatenate(
        [
            jnp.sum(jnp.where(which == k * blocks + row0, every, 0.0), axis=0, keepdims=True)
            for k in range(2)
        ],
        axis=0,
    )
    obs_wide[pl.ds(0, 2)] = picked
    rolled = pltpu.roll(obs_wide[...], (128 - lane0) % 128, 1)
    res[...] = rolled[0:2, 0:8] - obs[...]
    outs.append(pltpu.make_async_copy(res, r_out, out_sem.at[3]))
    outs[3].start()

    done = [c for pair in got_b1 for c in pair]
    for c in sent:
        if not any(c is d for d in done):
            c.wait_send()
    for c in outs:
        c.wait()


def store(*refs):
    given, given_back, held, sems = refs[:4], refs[4:8], refs[8:12], refs[12]
    loads = [pltpu.make_async_copy(a, b, sems.at[0, i]) for i, (a, b) in enumerate(zip(given, held))]
    stores = [pltpu.make_async_copy(a, b, sems.at[1, i]) for i, (a, b) in enumerate(zip(held, given_back))]
    for c in loads:
        c.start()
    for c, d in zip(loads, stores):
        c.wait()
        d.start()
    for c in stores:
        c.wait()


def solution(mesh):
    n_shot, n_space = mesh.shape["shot"], mesh.shape["space"]
    sizes = (n_shot, n_space, 4, 2, n_space // 8)

    def per_device(v, pm, p0, am, a0, cell, wave, cells, weights, obs):
        rows, ny, nz = v.shape
        traces = weights.shape[1]
        slab = (rows, ny, nz)
        hbm = pl.BlockSpec(memory_space=pltpu.HBM)
        vm = lambda *shape: pltpu.VMEM(shape, F32)
        count = 8 * CHUNKS + 2 + 4 + 2 * (sizes[2] + sizes[3] + sizes[4] - 3) + n_shot - 1
        results = (
                jax.ShapeDtypeStruct(slab, F32),
                jax.ShapeDtypeStruct(slab, F32),
                jax.ShapeDtypeStruct((2, 8), F32),
                jax.ShapeDtypeStruct((rows, ny // n_shot, nz), F32),
            )
        out = pl.pallas_call(
            functools.partial(kernel, sizes),
            out_shape=results,
            in_specs=[hbm] * 10,
            out_specs=[hbm] * 4,
            scratch_shapes=[vm(*slab)] * 12
            + [vm(2, 8), vm(rows, ny // n_shot, nz)]
            + [
                pltpu.VMEM((1, 1), jnp.int32),
                vm(1, 2),
                pltpu.VMEM((8, traces), jnp.int32),
                vm(8, traces),
                vm(2, 8),
                vm(8, 128),
                vm(4, 2, 4, ny, nz),
                vm(2, 4, ny, nz),
                pltpu.VMEM((2 * nz, traces), BF16),
                pltpu.VMEM((2 * traces, nz), BF16),
                pltpu.VMEM((ny, traces), BF16),
                vm(rows + 8, traces),
                vm(rows + 8, traces),
                vm(2, 4, traces),
                vm(2, 4, traces),
                pltpu.VMEM((2 * nz, nz), BF16),
                pltpu.VMEM((ny, 2 * ny), BF16),
                vm(8, 128),
                vm(4, 8, 128),
                vm(8, 128),
                vm(6, 8, 128),
                vm(2, sizes[4] - 1, 8, 128),
                vm(2, sizes[3] - 1, 8, 128),
                vm(2, sizes[2] - 1, 8, 128),
                vm(n_shot - 1, rows, ny // n_shot, nz),
                pltpu.SemaphoreType.DMA((10,)),
                pltpu.SemaphoreType.DMA((4,)),
                pltpu.SemaphoreType.DMA((count,)),
                pltpu.SemaphoreType.DMA((count,)),
            ],
            compiler_params=pltpu.CompilerParams(collective_id=0, has_side_effects=True, vmem_limit_bytes=56 << 20),
            cost_estimate=pl.CostEstimate(flops=10**9, bytes_accessed=2 << 20, transcendentals=0),
            name="two_steps",
        )(
            v, pm[0], p0[0], am[0], a0[0], cell.reshape(1, 1), wave,
            jnp.transpose(cells[0]), jnp.transpose(weights[0]), obs[0],
        )
        f, a, r, g = pl.pallas_call(
            store,
            out_shape=results,
            in_specs=[hbm] * 4,
            out_specs=[hbm] * 4,
            scratch_shapes=[vm(*r.shape) for r in results] + [pltpu.SemaphoreType.DMA((2, 4))],
            name="store",
        )(*out)
        return f[None], a[None], r[None], g

    field = P("shot", "space", None, None)
    return jax.shard_map(
        per_device,
        mesh=mesh,
        in_specs=(
            P("space", None, None), field, field, field, field,
            P("shot"), P("shot", None), P("shot", None, None), P("shot", None, None), P("shot", None, "space"),
        ),
        out_specs=(field, field, P("shot", None, "space"), P("space", "shot", None)),
        check_vma=False,
    )
```

```python
import functools

import jax
import jax.numpy as jnp
from jax import lax
from jax.experimental import pallas as pl
from jax.experimental.pallas import tpu as pltpu
from jax.sharding import PartitionSpec as P

MESH = pl.DeviceIdType.MESH
F32, BF16 = jnp.float32, jnp.bfloat16
coeffs = (-205.0 / 72.0, 8.0 / 5.0, -1.0 / 5.0, 8.0 / 315.0, -1.0 / 560.0)
whole = (8064.0, -1008.0, 128.0, -9.0)


CHUNKS = 1


def split(f):
    hi = f.astype(BF16)
    return hi, (f - hi.astype(F32)).astype(BF16)


def dot(a, b):
    return jnp.dot(a, b, preferred_element_type=F32)


def band(i, j):
    d = jnp.abs(i - j)
    m = jnp.zeros(d.shape, F32)
    for k, c in enumerate(whole):
        m = jnp.where(d == k + 1, c, m)
    return m.astype(BF16)


def iota(shape, dim):
    return lax.broadcasted_iota(jnp.int32, shape, dim)


def lap_inside(f, dz, dy):
    rows, ny, nz = f.shape
    hi, lo = split(f)
    zz = dot(jnp.concatenate([hi.reshape(rows * ny, nz), lo.reshape(rows * ny, nz)], axis=1), dz)
    yy = dot(dy, jnp.concatenate([jnp.concatenate([hi[x], lo[x]], axis=0) for x in range(rows)], axis=1))
    out = []
    for x in range(rows):
        r = 3.0 * coeffs[0] * f[x] + (zz[x * ny : (x + 1) * ny] + yy[:, x * nz : (x + 1) * nz]) * (1.0 / 5040.0)
        for j in range(1, 5):
            terms = [f[k] for k in (x - j, x + j) if 0 <= k < rows]
            if terms:
                r = r + coeffs[j] * functools.reduce(jnp.add, terms)
        out.append(r)
    return out


def from_left(h, i, edge):
    return functools.reduce(jnp.add, [(coeffs[j] * edge) * h[4 + i - j] for j in range(i + 1, 5)])


def from_right(h, i, edge):
    return functools.reduce(jnp.add, [(coeffs[j] * edge) * h[i + j - 4] for j in range(4 - i, 5)])


def kernel(
    sizes,
    v_in, pm_in, p0_in, am_in, a0_in, cell_in, wave_in, cells_in, weights_in, obs_in,
    P2, A2, res, grad,
    V, PM, P0, AM, A0, LAP0, P1, LAP1, A1, terms,
    cell, wave, cells, weights, obs, obs_wide,
    halo, outer, ozT, oz, oyT, wx, wv, vs, vs_in, dz, dy,
    part, part_in, arow, sums, sums_y, sums_z, sums_x, gin,
    load_sem, send_sem, recv_sem,
):
    n_shot, n_space, nx_, nz_, ny_ = sizes
    rows, ny, nz = V.shape
    traces = weights.shape[1]
    blocks = traces // 128
    h = lax.axis_index("shot")
    s = lax.axis_index("space")
    x, zh, y = s % nx_, (s // nx_) % nz_, s // (nx_ * nz_)

    def ring(k):
        return (h, (s + k + n_space) % n_space)

    def slab(x, zh, y):
        return (h, (y * nz_ + zh) * nx_ + x)

    to_y = [slab(x, zh, (y + k) % ny_) for k in range(1, ny_)]
    to_z = [slab(x, (zh + k) % nz_, y) for k in range(1, nz_)]
    to_x = [slab((x + k) % nx_, zh, y) for k in range(1, nx_)]
    to_shot = [((h + k) % n_shot, s) for k in range(1, n_shot)]
    near = [ring(1), ring(-1), ring(2), ring(-2)]

    barrier = pltpu.get_barrier_semaphore()
    partners = near + to_z + to_y + to_x + to_shot
    for d in partners:
        pl.semaphore_signal(barrier, inc=1, device_id=d, device_id_type=MESH)

    loads = [
        pltpu.make_async_copy(a, b, load_sem.at[i])
        for i, (a, b) in enumerate(
            (
                (cells_in, cells), (weights_in, weights), (p0_in, P0), (v_in, V), (pm_in, PM),
                (cell_in, cell), (wave_in, wave), (a0_in, A0), (am_in, AM), (obs_in, obs),
            )
        )
    ]
    for c in loads:
        c.start()

    sent = []

    def send(src, dst, to):
        i = len(sent)
        c = pltpu.make_async_remote_copy(
            src_ref=src, dst_ref=dst, send_sem=send_sem.at[i], recv_sem=recv_sem.at[i], device_id=to, device_id_type=MESH
        )
        c.start()
        sent.append(c)
        return c

    lo4, hi4 = pl.ds(0, 4), pl.ds(rows - 4, 4)

    dz[...] = band(iota((2 * nz, nz), 0) % nz, iota((2 * nz, nz), 1))
    dy[...] = band(iota((ny, 2 * ny), 0), iota((ny, 2 * ny), 1) % ny)

    loads[0].wait()
    loads[1].wait()
    at = cells[...]
    at_z = at[0:1] & (nz - 1)
    at_y = (at[0:1] // nz) & (ny - 1)
    hot = jnp.where(iota((nz, traces), 0) == at_z, 1.0, 0.0)
    ozT[pl.ds(0, nz)] = hot.astype(BF16)
    ozT[pl.ds(nz, nz)] = hot.astype(BF16)
    hot_t = jnp.transpose(hot).astype(BF16)
    oz[pl.ds(0, traces)] = hot_t
    oz[pl.ds(traces, traces)] = hot_t
    oyT[...] = jnp.where(iota((ny, traces), 0) == at_y, 1.0, 0.0).astype(BF16)
    at_x = at // (nz * ny) - s * rows + 4
    w = weights[...]
    acc = jnp.zeros((rows + 8, traces), F32)
    row_id = iota((rows + 8, traces), 0)
    for k in range(at.shape[0]):
        acc = acc + jnp.where(at_x[k : k + 1] == row_id, w[k : k + 1], 0.0)
    wx[...] = acc

    left_edge = jnp.where(s > 0, 1.0, 0.0).astype(F32)
    right_edge = jnp.where(s < n_space - 1, 1.0, 0.0).astype(F32)

    def at_traces(f):
        hi, lo = split(f)
        g = dot(jnp.concatenate([hi.reshape(rows * ny, nz), lo.reshape(rows * ny, nz)], axis=1), ozT[...])
        return [g[i * ny : (i + 1) * ny] for i in range(rows)]

    def over_y(g):
        return jnp.sum(g * oyT[...].astype(F32), axis=0, keepdims=True)

    for k in (2, 3, 4, 5, 6):
        loads[k].wait()
    place = cell[...] - s * (rows * ny * nz)
    flat = iota((ny, nz), 0) * nz + iota((ny, nz), 1)
    spots = [jnp.where(flat + i * (ny * nz) == place, 1.0, 0.0) for i in range(rows)]
    p0 = P0[...]
    lap = lap_inside(p0, dz[...], dy[...])
    for i in range(rows):
        LAP0[i] = lap[i]
        P1[i] = 2.0 * p0[i] - PM[i] + V[i] * (lap[i] + spots[i] * wave[0:1, 0:1])
    loads[7].wait()
    loads[8].wait()
    a0 = A0[...]
    lap = lap_inside(a0, dz[...], dy[...])
    for i in range(rows):
        A1[i] = 2.0 * a0[i] - AM[i] + V[i] * lap[i]

    for i, g in enumerate(at_traces(V[...])):
        vs[i // 4, pl.ds(i % 4, 1)] = over_y(g)

    loads[9].wait()
    lane0, row0 = (s * 8) % 128, (s * 8) // 128
    obs_wide[...] = jnp.zeros(obs_wide.shape, F32)
    obs_wide[pl.ds(0, 2), pl.ds(0, 8)] = obs[...]
    rolled = pltpu.roll(obs_wide[...], lane0, 1)
    which = iota((8, 128), 0)
    sums[0] = jnp.where(which == row0, rolled[0:1], 0.0) + jnp.where(which == blocks + row0, rolled[1:2], 0.0)

    pl.semaphore_wait(barrier, len(partners))

    wide = ny // CHUNKS
    parts = [pl.ds(c * wide, wide) for c in range(CHUNKS)]

    def exchange(field, low, high, c):
        a = send(low.at[:, parts[c]], halo.at[field, 1, :, parts[c]], ring(-1))
        b = send(high.at[:, parts[c]], halo.at[field, 0, :, parts[c]], ring(1))
        return b, a

    got_p0 = [exchange(0, P0.at[lo4], P0.at[hi4], c) for c in range(CHUNKS)]
    obs_y = [send(sums.at[0], sums_y.at[0, k], d) for k, d in enumerate(to_y)]
    got_a0 = [exchange(1, A0.at[lo4], A0.at[hi4], c) for c in range(CHUNKS)]
    vs_right = send(vs.at[0], vs_in.at[1], ring(-1))
    vs_left = send(vs.at[1], vs_in.at[0], ring(1))

    def gather(got, own, ref, slot, count):
        total = own
        for c in got:
            c.wait_recv()
        for k in range(count):
            total = total + ref[slot, k]
        return total

    sums[1] = gather(obs_y, sums[0], sums_y, 0, ny_ - 1)
    obs_z = [send(sums.at[1], sums_z.at[0, k], d) for k, d in enumerate(to_z)]

    got_p1 = []
    for c, ys in enumerate(parts):
        got_p0[c][0].wait_recv()
        hl = halo[0, 0, :, ys]
        for i in range(4):
            add = from_left(hl, i, left_edge)
            LAP0[i, ys] += add
            P1[i, ys] += V[i, ys] * add
        got_p0[c][1].wait_recv()
        hr = halo[0, 1, :, ys]
        for i in range(4):
            k = rows - 4 + i
            add = from_right(hr, i, right_edge)
            LAP0[k, ys] += add
            P1[k, ys] += V[k, ys] * add
        got_p1.append(exchange(2, P1.at[lo4], P1.at[hi4], c))

    p1 = P1[...]
    lines = [over_y(g) for g in at_traces(p1)]
    lap = lap_inside(p1, dz[...], dy[...])
    for i in range(rows):
        LAP1[i] = lap[i]
        P2[i] = 2.0 * p1[i] - P0[i] + V[i] * (lap[i] + spots[i] * wave[0:1, 1:2])
    acc = functools.reduce(jnp.add, [wx[4 + i : 5 + i] * g for i, g in enumerate(at_traces(P2[...]))])
    second = over_y(acc)
    first = functools.reduce(jnp.add, [wx[4 + i : 5 + i] * lines[i] for i in range(rows)])
    vs_left.wait_recv()
    vs_right.wait_recv()
    wv[pl.ds(0, 4)] = wx[0:4] * vs_in[0]
    wv[pl.ds(4, 4)] = wx[4:8] * vs[0]
    wv[pl.ds(8, 4)] = wx[8:12] * vs[1]
    wv[pl.ds(12, 4)] = wx[12:16] * vs_in[1]
    for i in range(4):
        second = second + wv[i : i + 1] * from_right(lines[0:4], i, 1.0)
        second = second + wv[rows + 4 + i : rows + 5 + i] * from_left(lines[rows - 4 :], i, 1.0)
    for k, line in enumerate((first, second)):
        for b in range(blocks):
            part[pl.ds(k * blocks + b, 1), :] = line[:, b * 128 : (b + 1) * 128]
    got_part = [send(part, part_in.at[i], d) for i, d in enumerate(near)]
    res_y = [send(part, sums_y.at[1, k], d) for k, d in enumerate(to_y)]

    got_b1 = []
    for c, ys in enumerate(parts):
        got_a0[c][0].wait_recv()
        hl = halo[1, 0, :, ys]
        for i in range(4):
            A1[i, ys] += V[i, ys] * from_left(hl, i, left_edge)
        got_a0[c][1].wait_recv()
        hr = halo[1, 1, :, ys]
        for i in range(4):
            k = rows - 4 + i
            A1[k, ys] += V[k, ys] * from_right(hr, i, right_edge)
        got_b1.append(exchange(3, A1.at[lo4], A1.at[hi4], c))

    sums[2] = gather(obs_z, sums[1], sums_z, 0, nz_ - 1)
    obs_x = [send(sums.at[2], sums_x.at[0, k], d) for k, d in enumerate(to_x)]

    for c, ys in enumerate(parts):
        got_p1[c][0].wait_recv()
        hl = halo[2, 0, :, ys]
        for i in range(4):
            add = from_left(hl, i, left_edge)
            LAP1[i, ys] += add
            P2[i, ys] += V[i, ys] * add
        got_p1[c][1].wait_recv()
        hr = halo[2, 1, :, ys]
        for i in range(4):
            k = rows - 4 + i
            add = from_right(hr, i, right_edge)
            LAP1[k, ys] += add
            P2[k, ys] += V[k, ys] * add

    sums[4] = gather(res_y, part[...], sums_y, 1, ny_ - 1)
    res_z = [send(sums.at[4], sums_z.at[1, k], d) for k, d in enumerate(to_z)]

    observed = gather(obs_x, sums[2], sums_x, 0, nx_ - 1)
    for c in got_part:
        c.wait_recv()
    arow[...] = functools.reduce(jnp.add, [part_in[i] for i in range(4)]) + part[...] - observed

    def inject(k, first, count):
        line = jnp.concatenate([arow[pl.ds(k * blocks + b, 1), :] for b in range(blocks)], axis=1)
        hi, lo = split(wv[pl.ds(first, count)] * line)
        hot = oyT[...]
        lhs = jnp.concatenate(
            [jnp.concatenate([hot * hi[i : i + 1], hot * lo[i : i + 1]], axis=1) for i in range(count)], axis=0
        )
        inj = dot(lhs, oz[...])
        return [inj[i * ny : (i + 1) * ny] for i in range(count)]

    for pair in got_b1:
        for c in pair:
            c.wait_send()
    inj = inject(1, 0, rows + 8)
    for i in range(4):
        outer[0, i] = inj[i]
        outer[1, i] = inj[rows + 4 + i]
    for i in range(rows):
        A1[i] += inj[4 + i]
    a1 = A1[...]
    inj = inject(0, 4, rows)
    lap = lap_inside(a1, dz[...], dy[...])
    scale = 1.0 / n_shot
    for i in range(rows):
        a2 = 2.0 * a1[i] - A0[i] + V[i] * lap[i] + inj[i]
        A2[i] = a2
        terms[i] = (a1[i] * LAP1[i] + a2 * LAP0[i]) * scale
    def finish_left():
        for c, ys in enumerate(parts):
            got_b1[c][0].wait_recv()
            hl = halo[3, 0, :, ys] * left_edge + outer[0, :, ys]
            for i in range(4):
                add = V[i, ys] * from_left(hl, i, 1.0)
                A2[i, ys] += add
                terms[i, ys] += add * LAP0[i, ys] * scale

    def finish_right():
        for c, ys in enumerate(parts):
            got_b1[c][1].wait_recv()
            hr = halo[3, 1, :, ys] * right_edge + outer[1, :, ys]
            for i in range(4):
                k = rows - 4 + i
                add = V[k, ys] * from_right(hr, i, 1.0)
                A2[k, ys] += add
                terms[k, ys] += add * LAP0[k, ys] * scale

    got_g = []
    for stage in range(2):
        right_now = (x == 0) if stage == 0 else (x != 0)
        pl.when(right_now)(finish_right)
        pl.when(jnp.logical_not(right_now))(finish_left)
        half = pl.ds(jnp.where(right_now, rows - 4, 0), 4)
        got_g += [
            send(terms.at[half, pl.ds(pl.multiple_of(d[0] * 8, 8), 8)], gin.at[k, half], d)
            for k, d in enumerate(to_shot)
        ]

    sums[5] = gather(res_z, sums[4], sums_z, 1, nz_ - 1)
    res_x = [send(sums.at[5], sums_x.at[1, k], d) for k, d in enumerate(to_x)]

    total = terms[:, pl.ds(pl.multiple_of(h * 8, 8), 8)]
    for c in got_g:
        c.wait_recv()
    for k in range(n_shot - 1):
        total = total + gin[k]
    grad[...] = total

    every = gather(res_x, sums[5], sums_x, 1, nx_ - 1)
    picked = jnp.concatenate(
        [
            jnp.sum(jnp.where(which == k * blocks + row0, every, 0.0), axis=0, keepdims=True)
            for k in range(2)
        ],
        axis=0,
    )
    obs_wide[pl.ds(0, 2)] = picked
    rolled = pltpu.roll(obs_wide[...], (128 - lane0) % 128, 1)
    res[...] = rolled[0:2, 0:8] - obs[...]

    done = [c for pair in got_b1 for c in pair]
    for c in sent:
        if not any(c is d for d in done):
            c.wait_send()


def store(*refs):
    copies = [pltpu.make_async_copy(a, b, refs[8].at[i]) for i, (a, b) in enumerate(zip(refs[:4], refs[4:8]))]
    for c in copies:
        c.start()
    for c in copies:
        c.wait()


def solution(mesh):
    n_shot, n_space = mesh.shape["shot"], mesh.shape["space"]
    sizes = (n_shot, n_space, 4, 2, n_space // 8)

    def per_device(v, pm, p0, am, a0, cell, wave, cells, weights, obs):
        rows, ny, nz = v.shape
        traces = weights.shape[1]
        slab = (rows, ny, nz)
        hbm = pl.BlockSpec(memory_space=pltpu.HBM)
        vmem = pl.BlockSpec(memory_space=pltpu.VMEM)
        vm = lambda *shape: pltpu.VMEM(shape, F32)
        count = 8 * CHUNKS + 2 + 4 + 2 * (sizes[2] + sizes[3] + sizes[4] - 3) + 2 * (n_shot - 1)
        results = (
                jax.ShapeDtypeStruct(slab, F32),
                jax.ShapeDtypeStruct(slab, F32),
                jax.ShapeDtypeStruct((2, 8), F32),
                jax.ShapeDtypeStruct((rows, ny // n_shot, nz), F32),
            )
        out = pl.pallas_call(
            functools.partial(kernel, sizes),
            out_shape=tuple(pltpu.VMEM(r.shape, F32) for r in results),
            in_specs=[hbm] * 10,
            out_specs=[vmem] * 4,
            scratch_shapes=[vm(*slab)] * 10
            + [
                pltpu.VMEM((1, 1), jnp.int32),
                vm(1, 2),
                pltpu.VMEM((8, traces), jnp.int32),
                vm(8, traces),
                vm(2, 8),
                vm(8, 128),
                vm(4, 2, 4, ny, nz),
                vm(2, 4, ny, nz),
                pltpu.VMEM((2 * nz, traces), BF16),
                pltpu.VMEM((2 * traces, nz), BF16),
                pltpu.VMEM((ny, traces), BF16),
                vm(rows + 8, traces),
                vm(rows + 8, traces),
                vm(2, 4, traces),
                vm(2, 4, traces),
                pltpu.VMEM((2 * nz, nz), BF16),
                pltpu.VMEM((ny, 2 * ny), BF16),
                vm(8, 128),
                vm(4, 8, 128),
                vm(8, 128),
                vm(6, 8, 128),
                vm(2, sizes[4] - 1, 8, 128),
                vm(2, sizes[3] - 1, 8, 128),
                vm(2, sizes[2] - 1, 8, 128),
                vm(n_shot - 1, rows, ny // n_shot, nz),
                pltpu.SemaphoreType.DMA((10,)),
                pltpu.SemaphoreType.DMA((count,)),
                pltpu.SemaphoreType.DMA((count,)),
            ],
            compiler_params=pltpu.CompilerParams(collective_id=0, has_side_effects=True, vmem_limit_bytes=40 << 20),
            cost_estimate=pl.CostEstimate(flops=10**9, bytes_accessed=2 << 20, transcendentals=0),
            name="two_steps",
        )(
            *(
                o if o.size == 1 else pltpu.with_memory_space_constraint(o, pltpu.HBM)
                for o in (
                    v, pm[0], p0[0], am[0], a0[0], cell.reshape(1, 1), wave,
                    jnp.transpose(cells[0]), jnp.transpose(weights[0]), obs[0],
                )
            )
        )
        f, a, r, g = pl.pallas_call(
            store,
            out_shape=results,
            in_specs=[vmem] * 4,
            out_specs=[hbm] * 4,
            scratch_shapes=[pltpu.SemaphoreType.DMA((4,))],
            name="store",
        )(*(pltpu.with_memory_space_constraint(o, pltpu.VMEM) for o in out))
        return f[None], a[None], r[None], g

    field = P("shot", "space", None, None)
    return jax.shard_map(
        per_device,
        mesh=mesh,
        in_specs=(
            P("space", None, None), field, field, field, field,
            P("shot"), P("shot", None), P("shot", None, None), P("shot", None, None), P("shot", None, "space"),
        ),
        out_specs=(field, field, P("shot", None, "space"), P("space", "shot", None)),
        check_vma=False,
    )
```

```python
import functools

import jax
import jax.numpy as jnp
from jax import lax
from jax.experimental import pallas as pl
from jax.experimental.pallas import tpu as pltpu
from jax.sharding import PartitionSpec as P

MESH = pl.DeviceIdType.MESH
F32, BF16 = jnp.float32, jnp.bfloat16
coeffs = (-205.0 / 72.0, 8.0 / 5.0, -1.0 / 5.0, 8.0 / 315.0, -1.0 / 560.0)
whole = (8064.0, -1008.0, 128.0, -9.0)


CHUNKS = 1


def split(f):
    hi = f.astype(BF16)
    return hi, (f - hi.astype(F32)).astype(BF16)


def dot(a, b):
    return jnp.dot(a, b, preferred_element_type=F32)


def band(i, j):
    d = jnp.abs(i - j)
    m = jnp.zeros(d.shape, F32)
    for k, c in enumerate(whole):
        m = jnp.where(d == k + 1, c, m)
    return m.astype(BF16)


def iota(shape, dim):
    return lax.broadcasted_iota(jnp.int32, shape, dim)


def lap_inside(f, dz, dy):
    rows, ny, nz = f.shape
    hi, lo = split(f)
    zz = dot(jnp.concatenate([hi.reshape(rows * ny, nz), lo.reshape(rows * ny, nz)], axis=1), dz)
    yy = dot(dy, jnp.concatenate([jnp.concatenate([hi[x], lo[x]], axis=0) for x in range(rows)], axis=1))
    out = []
    for x in range(rows):
        r = 3.0 * coeffs[0] * f[x] + (zz[x * ny : (x + 1) * ny] + yy[:, x * nz : (x + 1) * nz]) * (1.0 / 5040.0)
        for j in range(1, 5):
            terms = [f[k] for k in (x - j, x + j) if 0 <= k < rows]
            if terms:
                r = r + coeffs[j] * functools.reduce(jnp.add, terms)
        out.append(r)
    return out


def from_left(h, i, edge):
    return functools.reduce(jnp.add, [(coeffs[j] * edge) * h[4 + i - j] for j in range(i + 1, 5)])


def from_right(h, i, edge):
    return functools.reduce(jnp.add, [(coeffs[j] * edge) * h[i + j - 4] for j in range(4 - i, 5)])


class Halo:
    def __init__(self, copy, sends, receives):
        self.copy, self.sends, self.receives = copy, sends, receives

    def wait_send(self):
        pl.when(self.sends)(self.copy.wait_send)

    def wait_recv(self):
        pl.when(self.receives)(self.copy.wait_recv)


def kernel(
    sizes,
    v_in, pm_in, p0_in, am_in, a0_in, cell_in, wave_in, cells_in, weights_in, obs_in,
    P2, A2, res, grad,
    V, PM, P0, AM, A0, LAP0, P1, LAP1, A1, terms,
    cell, wave, cells, weights, obs, obs_wide,
    halo, outer, ozT, oz, oyT, wx, wv, vs, vs_in, dz, dy,
    part, part_in, arow, sums, sums_y, sums_z, sums_x, gin,
    load_sem, send_sem, recv_sem,
):
    n_shot, n_space, nx_, nz_, ny_ = sizes
    rows, ny, nz = V.shape
    traces = weights.shape[1]
    blocks = traces // 128
    h = lax.axis_index("shot")
    s = lax.axis_index("space")
    x, zh, y = s % nx_, (s // nx_) % nz_, s // (nx_ * nz_)

    def ring(k):
        return (h, (s + k + n_space) % n_space)

    def slab(x, zh, y):
        return (h, (y * nz_ + zh) * nx_ + x)

    to_y = [slab(x, zh, (y + k) % ny_) for k in range(1, ny_)]
    to_z = [slab(x, (zh + k) % nz_, y) for k in range(1, nz_)]
    to_x = [slab((x + k) % nx_, zh, y) for k in range(1, nx_)]
    to_shot = [((h + k) % n_shot, s) for k in range(1, n_shot)]
    near = [ring(1), ring(-1), ring(2), ring(-2)]

    barrier = pltpu.get_barrier_semaphore()
    has = [s < n_space - 1, s > 0, s < n_space - 2, s > 1]
    comes = [has[1], has[0], has[3], has[2]]
    for d, there in zip(near, has):
        pl.when(there)(lambda d=d: pl.semaphore_signal(barrier, inc=1, device_id=d, device_id_type=MESH))
    partners = to_z + to_y + to_x + to_shot
    for d in partners:
        pl.semaphore_signal(barrier, inc=1, device_id=d, device_id_type=MESH)

    loads = [
        pltpu.make_async_copy(a, b, load_sem.at[i])
        for i, (a, b) in enumerate(
            (
                (cells_in, cells), (weights_in, weights), (p0_in, P0), (v_in, V), (pm_in, PM),
                (cell_in, cell), (wave_in, wave), (a0_in, A0), (am_in, AM), (obs_in, obs),
            )
        )
    ]
    for c in loads:
        c.start()

    sent = []

    def send(src, dst, to):
        i = len(sent)
        c = pltpu.make_async_remote_copy(
            src_ref=src, dst_ref=dst, send_sem=send_sem.at[i], recv_sem=recv_sem.at[i], device_id=to, device_id_type=MESH
        )
        c.start()
        sent.append(c)
        return c

    lo4, hi4 = pl.ds(0, 4), pl.ds(rows - 4, 4)

    dz[...] = band(iota((2 * nz, nz), 0) % nz, iota((2 * nz, nz), 1))
    dy[...] = band(iota((ny, 2 * ny), 0), iota((ny, 2 * ny), 1) % ny)

    loads[0].wait()
    loads[1].wait()
    at = cells[...]
    at_z = at[0:1] & (nz - 1)
    at_y = (at[0:1] // nz) & (ny - 1)
    hot = jnp.where(iota((nz, traces), 0) == at_z, 1.0, 0.0)
    ozT[pl.ds(0, nz)] = hot.astype(BF16)
    ozT[pl.ds(nz, nz)] = hot.astype(BF16)
    hot_t = jnp.transpose(hot).astype(BF16)
    oz[pl.ds(0, traces)] = hot_t
    oz[pl.ds(traces, traces)] = hot_t
    oyT[...] = jnp.where(iota((ny, traces), 0) == at_y, 1.0, 0.0).astype(BF16)
    at_x = at // (nz * ny) - s * rows + 4
    w = weights[...]
    acc = jnp.zeros((rows + 8, traces), F32)
    row_id = iota((rows + 8, traces), 0)
    for k in range(at.shape[0]):
        acc = acc + jnp.where(at_x[k : k + 1] == row_id, w[k : k + 1], 0.0)
    wx[...] = acc

    for side, end in ((0, s == 0), (1, s == n_space - 1)):

        @pl.when(end)
        def _(side=side):
            for field in range(4):
                halo[field, side] = jnp.zeros((4, ny, nz), F32)
            vs_in[side] = jnp.zeros((4, traces), F32)

    for i in range(4):

        @pl.when(jnp.logical_not(comes[i]))
        def _(i=i):
            part_in[i] = jnp.zeros((8, 128), F32)

    left_edge = jnp.where(s > 0, 1.0, 0.0).astype(F32)
    right_edge = jnp.where(s < n_space - 1, 1.0, 0.0).astype(F32)

    def at_traces(f):
        hi, lo = split(f)
        g = dot(jnp.concatenate([hi.reshape(rows * ny, nz), lo.reshape(rows * ny, nz)], axis=1), ozT[...])
        return [g[i * ny : (i + 1) * ny] for i in range(rows)]

    def over_y(g):
        return jnp.sum(g * oyT[...].astype(F32), axis=0, keepdims=True)

    for k in (2, 3, 4, 5, 6):
        loads[k].wait()
    place = cell[...] - s * (rows * ny * nz)
    flat = iota((ny, nz), 0) * nz + iota((ny, nz), 1)
    spots = [jnp.where(flat + i * (ny * nz) == place, 1.0, 0.0) for i in range(rows)]
    p0 = P0[...]
    lap = lap_inside(p0, dz[...], dy[...])
    for i in range(rows):
        LAP0[i] = lap[i]
        P1[i] = 2.0 * p0[i] - PM[i] + V[i] * (lap[i] + spots[i] * wave[0:1, 0:1])
    loads[7].wait()
    loads[8].wait()
    a0 = A0[...]
    lap = lap_inside(a0, dz[...], dy[...])
    for i in range(rows):
        A1[i] = 2.0 * a0[i] - AM[i] + V[i] * lap[i]

    for i, g in enumerate(at_traces(V[...])):
        vs[i // 4, pl.ds(i % 4, 1)] = over_y(g)

    loads[9].wait()
    lane0, row0 = (s * 8) % 128, (s * 8) // 128
    obs_wide[...] = jnp.zeros(obs_wide.shape, F32)
    obs_wide[pl.ds(0, 2), pl.ds(0, 8)] = obs[...]
    rolled = pltpu.roll(obs_wide[...], lane0, 1)
    which = iota((8, 128), 0)
    sums[0] = jnp.where(which == row0, rolled[0:1], 0.0) + jnp.where(which == blocks + row0, rolled[1:2], 0.0)

    pl.semaphore_wait(barrier, len(partners) + sum(jnp.where(there, 1, 0) for there in has))

    wide = ny // CHUNKS
    parts = [pl.ds(c * wide, wide) for c in range(CHUNKS)]

    def between(src, dst, to, sends, receives):
        i = len(sent)
        copy = pltpu.make_async_remote_copy(
            src_ref=src, dst_ref=dst, send_sem=send_sem.at[i], recv_sem=recv_sem.at[i], device_id=to, device_id_type=MESH
        )
        sent.append(Halo(copy, sends, receives))
        pl.when(sends)(copy.start)
        return sent[-1]

    def exchange(field, low, high, c):
        a = between(low.at[:, parts[c]], halo.at[field, 1, :, parts[c]], ring(-1), s > 0, s < n_space - 1)
        b = between(high.at[:, parts[c]], halo.at[field, 0, :, parts[c]], ring(1), s < n_space - 1, s > 0)
        return b, a

    got_p0 = [exchange(0, P0.at[lo4], P0.at[hi4], c) for c in range(CHUNKS)]
    obs_y = [send(sums.at[0], sums_y.at[0, k], d) for k, d in enumerate(to_y)]
    got_a0 = [exchange(1, A0.at[lo4], A0.at[hi4], c) for c in range(CHUNKS)]
    vs_right = between(vs.at[0], vs_in.at[1], ring(-1), has[1], has[0])
    vs_left = between(vs.at[1], vs_in.at[0], ring(1), has[0], has[1])

    def gather(got, own, ref, slot, count):
        total = own
        for c in got:
            c.wait_recv()
        for k in range(count):
            total = total + ref[slot, k]
        return total

    sums[1] = gather(obs_y, sums[0], sums_y, 0, ny_ - 1)
    obs_z = [send(sums.at[1], sums_z.at[0, k], d) for k, d in enumerate(to_z)]

    got_p1 = []
    for c, ys in enumerate(parts):
        got_p0[c][0].wait_recv()
        hl = halo[0, 0, :, ys]
        for i in range(4):
            add = from_left(hl, i, left_edge)
            LAP0[i, ys] += add
            P1[i, ys] += V[i, ys] * add
        got_p0[c][1].wait_recv()
        hr = halo[0, 1, :, ys]
        for i in range(4):
            k = rows - 4 + i
            add = from_right(hr, i, right_edge)
            LAP0[k, ys] += add
            P1[k, ys] += V[k, ys] * add
        got_p1.append(exchange(2, P1.at[lo4], P1.at[hi4], c))

    p1 = P1[...]
    lines = [over_y(g) for g in at_traces(p1)]
    lap = lap_inside(p1, dz[...], dy[...])
    for i in range(rows):
        LAP1[i] = lap[i]
        P2[i] = 2.0 * p1[i] - P0[i] + V[i] * (lap[i] + spots[i] * wave[0:1, 1:2])
    acc = functools.reduce(jnp.add, [wx[4 + i : 5 + i] * g for i, g in enumerate(at_traces(P2[...]))])
    second = over_y(acc)
    first = functools.reduce(jnp.add, [wx[4 + i : 5 + i] * lines[i] for i in range(rows)])
    vs_left.wait_recv()
    vs_right.wait_recv()
    wv[pl.ds(0, 4)] = wx[0:4] * vs_in[0]
    wv[pl.ds(4, 4)] = wx[4:8] * vs[0]
    wv[pl.ds(8, 4)] = wx[8:12] * vs[1]
    wv[pl.ds(12, 4)] = wx[12:16] * vs_in[1]
    for i in range(4):
        second = second + wv[i : i + 1] * from_right(lines[0:4], i, 1.0)
        second = second + wv[rows + 4 + i : rows + 5 + i] * from_left(lines[rows - 4 :], i, 1.0)
    for k, line in enumerate((first, second)):
        for b in range(blocks):
            part[pl.ds(k * blocks + b, 1), :] = line[:, b * 128 : (b + 1) * 128]
    got_part = [between(part, part_in.at[i], d, has[i], comes[i]) for i, d in enumerate(near)]
    res_y = [send(part, sums_y.at[1, k], d) for k, d in enumerate(to_y)]

    got_b1 = []
    for c, ys in enumerate(parts):
        got_a0[c][0].wait_recv()
        hl = halo[1, 0, :, ys]
        for i in range(4):
            A1[i, ys] += V[i, ys] * from_left(hl, i, left_edge)
        got_a0[c][1].wait_recv()
        hr = halo[1, 1, :, ys]
        for i in range(4):
            k = rows - 4 + i
            A1[k, ys] += V[k, ys] * from_right(hr, i, right_edge)
        got_b1.append(exchange(3, A1.at[lo4], A1.at[hi4], c))

    sums[2] = gather(obs_z, sums[1], sums_z, 0, nz_ - 1)
    obs_x = [send(sums.at[2], sums_x.at[0, k], d) for k, d in enumerate(to_x)]

    for c, ys in enumerate(parts):
        got_p1[c][0].wait_recv()
        hl = halo[2, 0, :, ys]
        for i in range(4):
            add = from_left(hl, i, left_edge)
            LAP1[i, ys] += add
            P2[i, ys] += V[i, ys] * add
        got_p1[c][1].wait_recv()
        hr = halo[2, 1, :, ys]
        for i in range(4):
            k = rows - 4 + i
            add = from_right(hr, i, right_edge)
            LAP1[k, ys] += add
            P2[k, ys] += V[k, ys] * add

    sums[4] = gather(res_y, part[...], sums_y, 1, ny_ - 1)
    res_z = [send(sums.at[4], sums_z.at[1, k], d) for k, d in enumerate(to_z)]

    observed = gather(obs_x, sums[2], sums_x, 0, nx_ - 1)
    for c in got_part:
        c.wait_recv()
    arow[...] = functools.reduce(jnp.add, [part_in[i] for i in range(4)]) + part[...] - observed

    def inject(k, first, count):
        line = jnp.concatenate([arow[pl.ds(k * blocks + b, 1), :] for b in range(blocks)], axis=1)
        hi, lo = split(wv[pl.ds(first, count)] * line)
        hot = oyT[...]
        lhs = jnp.concatenate(
            [jnp.concatenate([hot * hi[i : i + 1], hot * lo[i : i + 1]], axis=1) for i in range(count)], axis=0
        )
        inj = dot(lhs, oz[...])
        return [inj[i * ny : (i + 1) * ny] for i in range(count)]

    for pair in got_b1:
        for c in pair:
            c.wait_send()
    inj = inject(1, 0, rows + 8)
    for i in range(4):
        outer[0, i] = inj[i]
        outer[1, i] = inj[rows + 4 + i]
    for i in range(rows):
        A1[i] += inj[4 + i]
    a1 = A1[...]
    inj = inject(0, 4, rows)
    lap = lap_inside(a1, dz[...], dy[...])
    scale = 1.0 / n_shot
    for i in range(rows):
        a2 = 2.0 * a1[i] - A0[i] + V[i] * lap[i] + inj[i]
        A2[i] = a2
        terms[i] = (a1[i] * LAP1[i] + a2 * LAP0[i]) * scale
    def finish_left():
        for c, ys in enumerate(parts):
            got_b1[c][0].wait_recv()
            hl = halo[3, 0, :, ys] * left_edge + outer[0, :, ys]
            for i in range(4):
                add = V[i, ys] * from_left(hl, i, 1.0)
                A2[i, ys] += add
                terms[i, ys] += add * LAP0[i, ys] * scale

    def finish_right():
        for c, ys in enumerate(parts):
            got_b1[c][1].wait_recv()
            hr = halo[3, 1, :, ys] * right_edge + outer[1, :, ys]
            for i in range(4):
                k = rows - 4 + i
                add = V[k, ys] * from_right(hr, i, 1.0)
                A2[k, ys] += add
                terms[k, ys] += add * LAP0[k, ys] * scale

    got_g = []
    for stage in range(2):
        right_now = (x == 0) if stage == 0 else (x != 0)
        pl.when(right_now)(finish_right)
        pl.when(jnp.logical_not(right_now))(finish_left)
        half = pl.ds(jnp.where(right_now, rows - 4, 0), 4)
        got_g += [
            send(terms.at[half, pl.ds(pl.multiple_of(d[0] * 8, 8), 8)], gin.at[k, half], d)
            for k, d in enumerate(to_shot)
        ]

    sums[5] = gather(res_z, sums[4], sums_z, 1, nz_ - 1)
    res_x = [send(sums.at[5], sums_x.at[1, k], d) for k, d in enumerate(to_x)]

    total = terms[:, pl.ds(pl.multiple_of(h * 8, 8), 8)]
    for c in got_g:
        c.wait_recv()
    for k in range(n_shot - 1):
        total = total + gin[k]
    grad[...] = total

    every = gather(res_x, sums[5], sums_x, 1, nx_ - 1)
    picked = jnp.concatenate(
        [
            jnp.sum(jnp.where(which == k * blocks + row0, every, 0.0), axis=0, keepdims=True)
            for k in range(2)
        ],
        axis=0,
    )
    obs_wide[pl.ds(0, 2)] = picked
    rolled = pltpu.roll(obs_wide[...], (128 - lane0) % 128, 1)
    res[...] = rolled[0:2, 0:8] - obs[...]

    done = [c for pair in got_b1 for c in pair]
    for c in sent:
        if not any(c is d for d in done):
            c.wait_send()


def store(*refs):
    copies = [pltpu.make_async_copy(a, b, refs[8].at[i]) for i, (a, b) in enumerate(zip(refs[:4], refs[4:8]))]
    for c in copies:
        c.start()
    for c in copies:
        c.wait()


def solution(mesh):
    n_shot, n_space = mesh.shape["shot"], mesh.shape["space"]
    sizes = (n_shot, n_space, 4, 2, n_space // 8)

    def per_device(v, pm, p0, am, a0, cell, wave, cells, weights, obs):
        rows, ny, nz = v.shape
        traces = weights.shape[1]
        slab = (rows, ny, nz)
        hbm = pl.BlockSpec(memory_space=pltpu.HBM)
        vmem = pl.BlockSpec(memory_space=pltpu.VMEM)
        vm = lambda *shape: pltpu.VMEM(shape, F32)
        count = 8 * CHUNKS + 2 + 4 + 2 * (sizes[2] + sizes[3] + sizes[4] - 3) + 2 * (n_shot - 1)
        results = (
                jax.ShapeDtypeStruct(slab, F32),
                jax.ShapeDtypeStruct(slab, F32),
                jax.ShapeDtypeStruct((2, 8), F32),
                jax.ShapeDtypeStruct((rows, ny // n_shot, nz), F32),
            )
        out = pl.pallas_call(
            functools.partial(kernel, sizes),
            out_shape=tuple(pltpu.VMEM(r.shape, F32) for r in results),
            in_specs=[hbm] * 10,
            out_specs=[vmem] * 4,
            scratch_shapes=[vm(*slab)] * 10
            + [
                pltpu.VMEM((1, 1), jnp.int32),
                vm(1, 2),
                pltpu.VMEM((8, traces), jnp.int32),
                vm(8, traces),
                vm(2, 8),
                vm(8, 128),
                vm(4, 2, 4, ny, nz),
                vm(2, 4, ny, nz),
                pltpu.VMEM((2 * nz, traces), BF16),
                pltpu.VMEM((2 * traces, nz), BF16),
                pltpu.VMEM((ny, traces), BF16),
                vm(rows + 8, traces),
                vm(rows + 8, traces),
                vm(2, 4, traces),
                vm(2, 4, traces),
                pltpu.VMEM((2 * nz, nz), BF16),
                pltpu.VMEM((ny, 2 * ny), BF16),
                vm(8, 128),
                vm(4, 8, 128),
                vm(8, 128),
                vm(6, 8, 128),
                vm(2, sizes[4] - 1, 8, 128),
                vm(2, sizes[3] - 1, 8, 128),
                vm(2, sizes[2] - 1, 8, 128),
                vm(n_shot - 1, rows, ny // n_shot, nz),
                pltpu.SemaphoreType.DMA((10,)),
                pltpu.SemaphoreType.DMA((count,)),
                pltpu.SemaphoreType.DMA((count,)),
            ],
            compiler_params=pltpu.CompilerParams(collective_id=0, has_side_effects=True, vmem_limit_bytes=40 << 20),
            cost_estimate=pl.CostEstimate(flops=10**9, bytes_accessed=2 << 20, transcendentals=0),
            name="two_steps",
        )(
            *(
                o if o.size == 1 else pltpu.with_memory_space_constraint(o, pltpu.HBM)
                for o in (
                    v, pm[0], p0[0], am[0], a0[0], cell.reshape(1, 1), wave,
                    jnp.transpose(cells[0]), jnp.transpose(weights[0]), obs[0],
                )
            )
        )
        f, a, r, g = pl.pallas_call(
            store,
            out_shape=results,
            in_specs=[vmem] * 4,
            out_specs=[hbm] * 4,
            scratch_shapes=[pltpu.SemaphoreType.DMA((4,))],
            name="store",
        )(*(pltpu.with_memory_space_constraint(o, pltpu.VMEM) for o in out))
        return f[None], a[None], r[None], g

    field = P("shot", "space", None, None)
    return jax.shard_map(
        per_device,
        mesh=mesh,
        in_specs=(
            P("space", None, None), field, field, field, field,
            P("shot"), P("shot", None), P("shot", None, None), P("shot", None, None), P("shot", None, "space"),
        ),
        out_specs=(field, field, P("shot", None, "space"), P("space", "shot", None)),
        check_vma=False,
    )
```
